32 devices in a mesh: group: 4 (over z), seq: 4 (over y, core), shard: 2 (over x).
Axes of the slice: x: 2, y: 2, z: 4, core: 2. Of those that a mesh axis runs over, the one named last changes fastest.
Arguments:
- text_rows: bfloat16 [4096, 8, 1280], P(('group', 'seq'), 'shard'), may hold values from -64 to 64
- vis_rows: bfloat16 [128, 8, 1280], P(('group', 'seq', 'shard')), may hold values from -6 to 6
- vis_dest: int32 [128, 1], P(('group', 'seq', 'shard')), may hold values from 0 to 3; in each aligned block of 8 rows (0 to 7, 8 to 15, ...) at most 4 rows name the same one
- segments: int32 [4352], P(('group', 'seq')), may hold values from 0 to 7, never falling along the last dimension, each value on 1 to 1088 neighbouring positions
Outputs:
- attended: bfloat16 [4352, 8, 1024], P(('group', 'seq'), 'shard')
The draws below stay inside these ranges and needn't reach their ends.
Inputs may be any that keep to these rules, and one draw needn't show every extreme that they name: `vis_dest`: in each aligned block of 8 rows (the visual rows listed by one index of group and seq, in device order), no value is named by more than 4 rows, and this bound is reached. `segments`: ids never fall along the sequence; each document covers 1 to 1088 positions, and one covers exactly 1088.
All inputs are finite; a program needn't handle non-finite values.
Results may differ from the reference program's by a relative error of at most 0.0028.
Values may be sent and summed in bfloat16 or wider, within the bound.
A program may use at most 64 MiB of HBM per device.

```python
import math
import jax
import jax.numpy as jnp
import numpy as np
from jax import lax

KVH = 8
GQ = 8
DH = 128
TEXT_DEV = 256
CAP = 4
REACH = 4
ROWS = 272
SLOTS = 4352
TEXT_ALL = 4096
VIS_DEV = 4
VIS_ALL = 128
DOCMAX = 1088
DOCS = 8
N_GROUP = 4
N_SEQ = 4
N_SHARD = 2


def draw_text_rows(key, part):
    row_width = (GQ + 2) * DH
    drawn = jax.random.normal(key, (TEXT_ALL, KVH, row_width), jnp.float32)
    spread = jnp.concatenate([jnp.full((GQ * DH,), 2.5, jnp.float32), jnp.ones((2 * DH,), jnp.float32)])
    result_rows = drawn * spread
    return result_rows.astype(jnp.bfloat16)


def level_of(rng, extent, shards, least, largest):
    level, own = 1.0, jax.random.fold_in(rng, 6)
    for position, parts in shards:
        draws = jnp.exp(jax.random.uniform(jax.random.fold_in(own, position), (parts,), jnp.float32, least / len(shards), largest / len(shards)))
        level = level * jnp.repeat(draws, extent[position] // parts).reshape([-1 if axis == position else 1 for axis in range(len(extent))])
    return level


def profile(number_of, total, reach, slope):
    loads = [(1 << 20) // math.isqrt(rank ** slope) + 1 for rank in range(2, number_of + 1)]
    surplus, counts = total - reach - (number_of - 1), [1] * (number_of - 1)
    while surplus > 0:
        movable = [i for i in range(number_of - 1) if counts[i] < reach]
        whole, remaining = sum([loads[i] for i in movable]), surplus
        for i in movable:
            addition = min(reach - counts[i], max(1, remaining * loads[i] // whole), surplus)
            counts[i] = counts[i] + addition
            surplus = surplus - addition
    return np.array([reach] + counts)


def uneven(stream_key, number_of, total, bound, lean):
    if number_of == 2:
        one = jax.random.randint(stream_key, (), max(1, total - bound), min(bound, total - 1) + 1)
        return jnp.stack([one, total - one])
    lengths = jnp.asarray(profile(number_of, total, bound, lean), jnp.int32)
    pairs = (number_of - 1) // 2
    source_of, taker = lengths[1:1 + 2 * pairs:2], lengths[2:2 + 2 * pairs:2]
    room = jnp.minimum(source_of - 1, bound - taker)
    shifted = jax.random.randint(jax.random.fold_in(stream_key, 1), (pairs,), 0, 1 << 20) % (room + 1)
    lengths = lengths.at[1:1 + 2 * pairs:2].set(source_of - shifted).at[2:2 + 2 * pairs:2].set(taker + shifted)
    return lengths[jax.random.permutation(jax.random.fold_in(stream_key, 2), number_of)]


def assign_block(stream_key, own, number, rows, number_of, top, limit, skew):
    sequence = jax.random.permutation(stream_key, number_of)
    heavy_load, usual = load_shares(number_of, rows * top, limit, skew, True), load_shares(number_of, rows * top, limit, skew, False)
    places = jnp.arange(number_of)

    def named(lengths, turn):
        used = int((lengths > 0).sum())
        fixed = max(1, used // 4)
        passed = fixed + (places - fixed + turn * (used - fixed)) % max(1, number_of - fixed)
        return jnp.zeros((number_of,), jnp.int32).at[sequence[jnp.where(places < fixed, places, passed)]].set(jnp.asarray(lengths, jnp.int32))

    lengths = jnp.where(number % 4 == 0, named(heavy_load, number // 4), named(usual, number - number // 4 - 1))
    mixed = jax.random.permutation(jax.random.fold_in(own, 3), number_of)
    giver, receiver = mixed[0:number_of // 2 * 2:2], mixed[1:number_of // 2 * 2:2]
    room = jnp.minimum(lengths[giver] - 1, limit - lengths[receiver]) // 2
    room = jnp.where((giver == sequence[0]) | (receiver == sequence[0]) | (lengths[receiver] == 0), 0, jnp.maximum(room, 0))
    passed = jax.random.randint(jax.random.fold_in(own, 4), (number_of // 2,), 0, 1 << 20) % (room + 1)
    lengths = lengths.at[giver].add(-passed).at[receiver].add(passed)
    members = jnp.searchsorted(jnp.cumsum(lengths), jnp.arange(rows * top), side="right").astype(jnp.int32)
    listing = members.reshape(top, rows).T
    listing = listing[jax.random.permutation(jax.random.fold_in(own, 1), rows)]
    turn = jax.random.randint(jax.random.fold_in(own, 2), (rows, 1), 0, top)
    return jnp.take_along_axis(listing, (jnp.arange(top)[None, :] + turn) % top, axis=1)


def load_shares(count, total, limit, lean, full):
    loads = [(1 << 20) // math.isqrt(grade ** lean) + 1 for grade in range(1, count + 1)]
    largest = limit if full else min(limit, max(-(-total // count), total * loads[0] // sum(loads)))
    least = 1 if total - largest >= count - 1 else 0
    given, spare = [largest] + [least] * (count - 1), total - largest - least * (count - 1)
    while spare > 0:
        free = [i for i in range(1, count) if given[i] < largest] or [i for i in range(1, count) if given[i] < limit]
        whole, remaining = sum([loads[i] for i in free]), spare
        for i in free:
            extra = min(limit - given[i], max(1, remaining * loads[i] // whole), spare)
            given[i] = given[i] + extra
            spare = spare - extra
    return np.array(given)


def normal_values(own_key, extent, scale, most, split=(), kind=jnp.bfloat16):
    gain = level_of(own_key, extent, split, -0.22, 0.18) if split else 1.0
    values = jax.random.normal(own_key, extent, jnp.float32) * scale * gain
    return jnp.minimum(jnp.maximum(values, -most), most).astype(kind)


def setup_inputs(seed: int = 0) -> dict:
    key_of = jax.random.split(jax.random.key(seed), 5)
    text_rows = draw_text_rows(jax.random.fold_in(key_of[4], 71), 0)
    vis_rows = normal_values(key_of[1], (VIS_ALL, KVH, (GQ + 2) * DH), 1.0, 6.0, ((0, 32),))
    vis_dest_keys = jax.random.split(jax.random.fold_in(key_of[2], 1), VIS_ALL // (N_SHARD * VIS_DEV))
    vis_dest_turns = jax.random.permutation(jax.random.fold_in(key_of[2], 3), VIS_ALL // (N_SHARD * VIS_DEV))
    vis_dest = jax.vmap(lambda own, number: assign_block(jax.random.fold_in(key_of[2], 2), own, number, N_SHARD * VIS_DEV, N_SEQ, 1, CAP, 2))(vis_dest_keys, vis_dest_turns).reshape((VIS_ALL, 1))
    segments = jnp.searchsorted(jnp.cumsum(uneven(key_of[3], DOCS, SLOTS, DOCMAX, 2)), jnp.arange(SLOTS), side="right").astype(jnp.int32)
    return dict(text_rows=text_rows, vis_rows=vis_rows, vis_dest=vis_dest, segments=segments)


def reference(text_rows, vis_rows, vis_dest, segments):
    blocks = N_GROUP * N_SEQ
    block_rows = N_SHARD * VIS_DEV
    slot_count = N_SEQ * CAP
    row_width = (GQ + 2) * DH
    target = vis_dest[:, 0].reshape(blocks, block_rows)
    onehot = (target[:, :, None] == jnp.arange(N_SEQ, dtype=jnp.int32)[None, None, :]).astype(jnp.int32)
    before = jnp.cumsum(onehot, axis=1) - onehot
    slot_rank = jnp.sum(before * onehot, axis=2)
    source = jnp.arange(blocks, dtype=jnp.int32)[:, None]
    owner_block = (source // N_SEQ) * N_SEQ + target
    flat_slot = ((owner_block * N_SEQ + source % N_SEQ) * CAP + slot_rank).reshape(-1).astype(jnp.int32)
    slot_rows = jnp.zeros((blocks * slot_count, KVH, row_width), vis_rows.dtype).at[flat_slot].set(vis_rows)
    filled = jnp.zeros((blocks * slot_count,), jnp.int32).at[flat_slot].set(1)
    seq_rows = jnp.concatenate([text_rows.reshape(blocks, TEXT_DEV, KVH, row_width), slot_rows.reshape(blocks, slot_count, KVH, row_width)], axis=1).reshape(blocks * ROWS, KVH, row_width)
    live_rows = jnp.concatenate([jnp.ones((blocks, TEXT_DEV), jnp.int32), filled.reshape(blocks, slot_count)], axis=1).reshape(-1)
    doc_tag = jnp.where(live_rows > 0, segments + 1, 0).astype(jnp.int32)
    margin = REACH * ROWS
    keyval = jnp.concatenate([jnp.zeros((margin, KVH, 2 * DH), seq_rows.dtype), seq_rows[:, :, GQ * DH:]], axis=0)
    tag_pad = jnp.concatenate([jnp.zeros((margin,), jnp.int32), doc_tag])
    key_place = jnp.arange((REACH + 1) * ROWS, dtype=jnp.int32) - margin
    row_place = jnp.arange(ROWS, dtype=jnp.int32)
    score_scale = DH ** -0.5

    def one_block(block_index):
        first_row = (block_index * ROWS).astype(jnp.int32)
        queries = lax.dynamic_slice_in_dim(seq_rows, first_row, ROWS, 0)[:, :, :GQ * DH]
        queries = queries.reshape(ROWS, KVH, GQ, DH).astype(jnp.float32)
        key_rows = lax.dynamic_slice_in_dim(keyval, first_row, (REACH + 1) * ROWS, 0).astype(jnp.float32)
        key_tags = lax.dynamic_slice_in_dim(tag_pad, first_row, (REACH + 1) * ROWS, 0)
        query_segs = lax.dynamic_slice_in_dim(segments, first_row, ROWS, 0)
        query_live = lax.dynamic_slice_in_dim(live_rows, first_row, ROWS, 0) > 0
        visible = (key_place[None, :] <= row_place[:, None]) & (key_tags[None, :] == (query_segs + 1)[:, None]) & query_live[:, None]
        scores = jnp.einsum("rgqd,kgd->gqrk", queries, key_rows[:, :, :DH]) * score_scale
        scores = jnp.where(visible[None, None], scores, -1e30)
        row_max = jnp.max(scores, axis=3, keepdims=True)
        weights = jnp.where(visible[None, None], jnp.exp(scores - row_max), 0.0)
        row_total = jnp.where(query_live[None, None, :], jnp.sum(weights, axis=3), 1.0)
        rounded = lax.optimization_barrier(weights.astype(jnp.bfloat16)).astype(jnp.float32)
        weighted = jnp.einsum("gqrk,kgd->gqrd", rounded, key_rows[:, :, DH:])
        result = (weighted / row_total[..., None]).astype(jnp.bfloat16)
        return result.transpose(2, 0, 1, 3).reshape(ROWS, KVH, GQ * DH)

    outputs = lax.map(one_block, jnp.arange(blocks, dtype=jnp.int32))
    return outputs.reshape(blocks * ROWS, KVH, GQ * DH)
```

```python
import functools
import math

import jax
import jax.numpy as jnp
import numpy as np
from jax import lax
from jax.experimental import pallas as pl
from jax.experimental.pallas import tpu as pltpu
from jax.sharding import PartitionSpec as P

GQ = 8
DH = 128
CAP = 4
REACH = 4
FAR = -1e30
LOG2E = math.log2(math.e)
MESH = pl.DeviceIdType.MESH


def up(value, step):
    return -(-value // step) * step


def kernel(
    n_group, n_seq, n_shard, text_ref, vis_ref, seg_row_ref, seg_col_ref, same_ref, pick_ref, slot_ref,
    out_ref, kv_buf, aux_buf, vis_buf, key_all, val_all, bias, slots, live_col,
    send_sem, recv_sem, vis_send, vis_recv,
):
    groups, text, width = text_ref.shape
    query_width = GQ * DH
    rows = out_ref.shape[1]
    slot_count = rows - text
    half = text // 2
    pad = key_all.shape[0] - (REACH + 1) * text
    slot_start = REACH * text + half
    vis_block = vis_ref.shape[1]
    n_source = n_seq * n_shard
    blocks = n_group * n_seq
    aux_rows = groups * slot_count

    my_group, my_seq, my_shard = lax.axis_index("group"), lax.axis_index("seq"), lax.axis_index("shard")
    here = my_group * n_seq + my_seq
    odd = lax.rem(here, 2)
    upper = lax.rem(here // 2, 2)
    sibling = here + 1 - 2 * odd
    partner = here + 2 - 4 * upper
    me = my_seq * n_shard + my_shard

    def device(block):
        return (block // n_seq, lax.rem(block, n_seq), my_shard)

    def peer(index):
        return (my_group, index // n_shard, lax.rem(index, n_shard))

    barrier = pltpu.get_barrier_semaphore()

    def greet(step, carry):
        pl.semaphore_signal(barrier, inc=1, device_id=peer(lax.rem(me + step, n_source)), device_id_type=MESH)
        return carry

    lax.fori_loop(1, n_source, greet, 0)
    pl.semaphore_signal(barrier, inc=1, device_id=device(sibling), device_id_type=MESH)
    pl.semaphore_signal(barrier, inc=1, device_id=device(partner), device_id_type=MESH)

    @pl.when(here >= REACH)
    def _():
        pl.semaphore_signal(barrier, inc=1, device_id=device(here - REACH), device_id_type=MESH)

    for place in range(REACH):
        @pl.when(here < REACH - place)
        def _():
            kv_buf[:, place] = jnp.zeros_like(kv_buf[:, place])
            aux_buf[place] = jnp.zeros_like(aux_buf[place])

    pl.semaphore_wait(barrier, n_source + 1 + (here + REACH < blocks).astype(jnp.int32))

    def landing(item, place):
        return aux_buf.at[place] if item == groups else kv_buf.at[item, place]

    def source(item, place):
        if place < REACH:
            return landing(item, place)
        if item == groups:
            return aux_buf.at[REACH]
        return text_ref.at[item, :, pl.ds(query_width, 2 * DH)]

    def transfer(item, number, place, target_place, target):
        return pltpu.make_async_remote_copy(
            src_ref=source(item, place),
            dst_ref=landing(item, target_place),
            send_sem=send_sem.at[item, number],
            recv_sem=recv_sem.at[item, target_place],
            device_id=device(target),
            device_id_type=MESH,
        )

    own_copies = [
        (here + REACH < blocks, 0, 4, 0, here + REACH),
        (upper == 0, 1, 4, 2, here + 2),
        (odd == 0, 2, 4, 3, here + 1),
    ]
    far_copies = [
        ((here >= 4) & (upper == 1), 3, 0, 2, here - 2),
        ((here >= 4) & (odd == 1), 4, 0, 1, here - 1),
    ]
    near_copies = [
        ((here >= 2) & (odd == 0), 5, 2, 1, here + 1),
        ((here >= 2) & (odd == 1), 5, 2, 3, here - 1),
    ]

    def start(item, copies):
        for condition, number, place, target_place, target in copies:
            @pl.when(condition)
            def _():
                transfer(item, number, place, target_place, target).start()

    def finish(item, copies):
        for condition, number, place, target_place, target in copies:
            @pl.when(condition)
            def _():
                transfer(item, number, place, target_place, target).wait_send()

    def arrive(item, place):
        @pl.when(here >= REACH - place)
        def _():
            transfer(item, 0, place, place, sibling).wait_recv()

    def relay_far(item):
        arrive(item, 0)
        start(item, far_copies)

    def relay_near(item):
        arrive(item, 2)
        start(item, near_copies)

    def vis_copy(step, landing_index):
        target = lax.rem(me + step, n_source)
        return pltpu.make_async_remote_copy(
            src_ref=vis_ref.at[lax.rem(target, n_shard)],
            dst_ref=vis_buf.at[landing_index],
            send_sem=vis_send.at[step],
            recv_sem=vis_recv.at[step],
            device_id=peer(target),
            device_id_type=MESH,
        )

    def vis_start(step, carry):
        vis_copy(step, me).start()
        return carry

    lax.fori_loop(1, n_source, vis_start, 0)
    for item in range(groups):
        start(item, own_copies)
    vis_buf[me] = vis_ref[my_shard]

    def vis_wait(step, carry):
        vis_copy(step, lax.rem(me + n_source - step, n_source)).wait_recv()
        return carry

    lax.fori_loop(1, n_source, vis_wait, 0)

    block_rows = n_shard * vis_block
    my_dest = my_seq.astype(jnp.float32)
    filled = jnp.zeros((aux_rows, 1), jnp.float32)
    for seq in range(n_seq):
        listed = vis_buf[seq * n_shard:(seq + 1) * n_shard].reshape(block_rows, width + DH)
        dest = listed[:, width:].astype(jnp.float32)
        dest_across = dest.T[0:1, :]
        earlier = jnp.where(dest[:, 0:1] == dest_across, same_ref[...], 0.0)
        rank = jnp.sum(earlier, axis=0, keepdims=True)
        placing = jnp.where(
            (slot_ref[...] == rank + float(seq * CAP)) & (dest_across == my_dest), pick_ref[...], 0.0
        )
        part = jnp.dot(placing.astype(jnp.bfloat16), listed[:, :width], preferred_element_type=jnp.float32)
        slots[...] = part if seq == 0 else slots[...] + part
        filled = filled + jnp.sum(placing, axis=1, keepdims=True)
    aux_buf[REACH, 0:aux_rows] = slots[:, query_width:].astype(jnp.bfloat16)
    live_col[...] = jnp.broadcast_to(filled[:slot_count], live_col.shape)
    live_across = live_col[...].T[0:1, :]
    seg_row = seg_row_ref[...].astype(jnp.float32) + 1.0
    text_tags = seg_row[:, :text]
    slot_tags = jnp.where(live_across > 0, seg_row[:, text:], 0.0)
    tag_rows = jnp.concatenate(
        [
            jnp.broadcast_to(text_tags, (8, text)),
            jnp.concatenate(
                [jnp.broadcast_to(slot_tags, (8, slot_count)), jnp.zeros((8, text - slot_count), jnp.float32)], axis=1
            ),
        ],
        axis=0,
    )
    aux_buf[REACH, aux_rows:] = tag_rows.astype(jnp.bfloat16)
    start(groups, own_copies)

    relay_far(0)
    relay_far(groups)
    relay_near(0)
    relay_near(groups)
    if groups > 1:
        relay_far(1)
    arrive(groups, 1)
    arrive(groups, 3)

    all_tags, all_places = [], []

    def lane_places(count):
        return lax.broadcasted_iota(jnp.int32, (1, count), 1)

    for place in range(REACH):
        all_tags.append(aux_buf[place, aux_rows:].astype(jnp.float32)[0:1, :])
        all_places.append(lane_places(text) - (REACH - place) * rows)
    slot_tag_list, slot_place_list = [], []
    for place in range(REACH + 1):
        slot_tag_list.append(aux_buf[place, aux_rows:].astype(jnp.float32)[8:9, :slot_count])
        slot_place_list.append(lane_places(slot_count) - (REACH - place) * rows + text)
    spare = pad - (REACH + 1) * slot_count
    if spare:
        slot_tag_list.append(jnp.zeros((1, spare), jnp.float32))
        slot_place_list.append(jnp.zeros((1, spare), jnp.int32))
    all_tags += [text_tags[:, :half]] + slot_tag_list + [text_tags[:, half:]]
    all_places += [lane_places(half)] + slot_place_list + [lane_places(half) + half]
    tags = jnp.concatenate(all_tags, axis=1)
    places = jnp.concatenate(all_places, axis=1)
    row_tags = seg_col_ref[...].astype(jnp.float32) + 1.0
    row_places = lax.broadcasted_iota(jnp.int32, (rows, 1), 0)
    for first in range(0, rows, 16):
        part = slice(first, first + 16)
        seen = (tags == row_tags[part]) & (places <= row_places[part])
        bias[part, :] = jnp.where(seen, 0.0, FAR)

    val_all[:, DH:] = jnp.ones_like(val_all[:, DH:])
    if spare:
        blank = jnp.zeros((spare, DH), jnp.bfloat16)
        key_all[slot_start + pad - spare:slot_start + pad, :] = blank
        val_all[slot_start + pad - spare:slot_start + pad, :DH] = blank
    scale = LOG2E * DH ** -0.5
    total = key_all.shape[0]

    def attend(queries, heads, rows_from, rows_to, low, high):
        count = rows_to - rows_from
        scores = lax.dot_general(
            queries, key_all[low:high], (((1,), (1,)), ((), ())), preferred_element_type=jnp.float32
        )
        scores = (scores.reshape(heads, count, high - low) + bias[rows_from:rows_to, low:high][None]).reshape(
            heads * count, high - low
        )
        largest = jnp.max(scores, axis=1, keepdims=True)
        weights = jnp.exp2((scores - largest) * scale).astype(jnp.bfloat16)
        summed = jnp.dot(weights, val_all[low:high], preferred_element_type=jnp.float32)
        return summed[:, :DH] / summed[:, DH:]

    together = 2
    for group in range(groups):
        arrive(group, 1)
        arrive(group, 3)
        for place in range(REACH):
            key_all[place * text:(place + 1) * text, :] = kv_buf[group, place, :, :DH]
            val_all[place * text:(place + 1) * text, :DH] = kv_buf[group, place, :, DH:]
        own = text_ref[group, :, query_width:]
        key_all[REACH * text:slot_start, :] = own[:half, :DH]
        val_all[REACH * text:slot_start, :DH] = own[:half, DH:]
        key_all[slot_start + pad:, :] = own[half:, :DH]
        val_all[slot_start + pad:, :DH] = own[half:, DH:]
        for place in range(REACH + 1):
            slot_rows = aux_buf[place, group * slot_count:(group + 1) * slot_count]
            at = slot_start + place * slot_count
            key_all[at:at + slot_count, :] = slot_rows[:, :DH]
            val_all[at:at + slot_count, :DH] = slot_rows[:, DH:]

        def some_heads(index, carry):
            lanes = [pl.ds(pl.multiple_of((index * together + k) * DH, DH), DH) for k in range(together)]
            for rows_from, low, high in ((0, 0, slot_start + pad), (half, half, total)):
                queries = jnp.concatenate(
                    [text_ref[group, rows_from:rows_from + half, lane] for lane in lanes], axis=0
                )
                result = attend(queries, together, rows_from, rows_from + half, low, high).astype(jnp.bfloat16)
                for k, lane in enumerate(lanes):
                    out_ref[group, rows_from:rows_from + half, lane] = result[k * half:(k + 1) * half]
            return carry

        steps = GQ // together
        lax.fori_loop(0, steps // 2, some_heads, 0)
        if group + 1 < groups:
            relay_near(group + 1)
            if group + 2 < groups:
                relay_far(group + 2)
        lax.fori_loop(steps // 2, steps, some_heads, 0)
        slot_queries = slots[group * slot_count:(group + 1) * slot_count, :query_width].astype(jnp.bfloat16)
        queries = jnp.concatenate([slot_queries[:, k * DH:(k + 1) * DH] for k in range(GQ)], axis=0)
        result = attend(queries, GQ, text, rows, text, total)
        live = live_col[...]
        for k in range(GQ):
            head = jnp.where(live > 0, result[k * slot_count:(k + 1) * slot_count], 0.0)
            out_ref[group, text:, k * DH:(k + 1) * DH] = head.astype(jnp.bfloat16)

    for item in range(groups + 1):
        finish(item, own_copies + far_copies + near_copies)

    def vis_finish(step, carry):
        vis_copy(step, me).wait_send()
        return carry

    lax.fori_loop(1, n_source, vis_finish, 0)


def shards(mesh_shape, text_rows, vis_rows, vis_dest, segments):
    n_group, n_seq, n_shard = (mesh_shape[axis] for axis in ("group", "seq", "shard"))
    text, groups, width = text_rows.shape
    rows = segments.shape[0]
    slot_count = n_seq * CAP
    vis_count = vis_rows.shape[0]
    vis_block = up(vis_count * groups, 16)
    text_t = text_rows.transpose(1, 0, 2)
    listed = jnp.concatenate(
        [
            vis_rows,
            jnp.broadcast_to(vis_dest[:, :, None].astype(jnp.bfloat16), (vis_count, vis_rows.shape[1], DH)),
        ],
        axis=2,
    )
    listed = listed.reshape(vis_count, n_shard, groups, width + DH).transpose(1, 0, 2, 3)
    listed = listed.reshape(n_shard, vis_count * groups, width + DH)
    listed = jnp.pad(listed, ((0, 0), (0, vis_block - vis_count * groups), (0, 0)))

    index = np.arange(n_shard * vis_block)
    within = index % vis_block
    valid = within < vis_count * groups
    head = within % groups
    same = (head[:, None] == head[None, :]) & (index[:, None] < index[None, :]) & valid[:, None] & valid[None, :]
    place = np.arange(groups * slot_count)
    pick = (place[:, None] // slot_count == head[None, :]) & valid[None, :]
    slot = np.broadcast_to((place % slot_count)[:, None], pick.shape)

    pad = up((REACH + 1) * slot_count, 128)
    keys = (REACH + 1) * text + pad
    aux_rows = groups * slot_count + 16
    n_source = n_seq * n_shard
    vmem = pl.BlockSpec(memory_space=pltpu.VMEM)
    result = pl.pallas_call(
        functools.partial(kernel, n_group, n_seq, n_shard),
        out_shape=jax.ShapeDtypeStruct((groups, rows, GQ * DH), jnp.bfloat16),
        in_specs=[vmem] * 7,
        out_specs=vmem,
        scratch_shapes=[
            pltpu.VMEM((groups, REACH, text, 2 * DH), jnp.bfloat16),
            pltpu.VMEM((REACH + 1, aux_rows, 2 * DH), jnp.bfloat16),
            pltpu.VMEM((n_source, vis_block, width + DH), jnp.bfloat16),
            pltpu.VMEM((keys, DH), jnp.bfloat16),
            pltpu.VMEM((keys, 2 * DH), jnp.bfloat16),
            pltpu.VMEM((rows, keys), jnp.float32),
            pltpu.VMEM((groups * slot_count, width), jnp.float32),
            pltpu.VMEM((slot_count, DH), jnp.float32),
            pltpu.SemaphoreType.DMA((groups + 1, 6)),
            pltpu.SemaphoreType.DMA((groups + 1, REACH)),
            pltpu.SemaphoreType.DMA((n_source,)),
            pltpu.SemaphoreType.DMA((n_source,)),
        ],
        compiler_params=pltpu.CompilerParams(
            collective_id=0, has_side_effects=True, vmem_limit_bytes=56 * 1024 * 1024
        ),
    )(
        text_t,
        listed,
        segments[None, :],
        segments[:, None],
        jnp.asarray(same, jnp.float32),
        jnp.asarray(pick, jnp.float32),
        jnp.asarray(slot, jnp.float32),
    )
    return result.transpose(1, 0, 2)


def solution(mesh):
    placed = (
        P(("group", "seq"), "shard", None),
        P(("group", "seq", "shard"), None, None),
        P(("group", "seq", "shard"), None),
        P(("group", "seq")),
    )
    return jax.shard_map(
        functools.partial(shards, dict(mesh.shape)),
        mesh=mesh,
        in_specs=placed,
        out_specs=P(("group", "seq"), "shard", None),
        check_vma=False,
    )
```

```python
import functools
import math

import jax
import jax.numpy as jnp
import numpy as np
from jax import lax
from jax.experimental import pallas as pl
from jax.experimental.pallas import tpu as pltpu
from jax.sharding import PartitionSpec as P

GQ = 8
DH = 128
CAP = 4
REACH = 4
FAR = -(2.0 ** 100)
OWN = 120
LOG2E = math.log2(math.e)
MESH = pl.DeviceIdType.MESH


def up(value, step):
    return -(-value // step) * step


def kernel(
    n_group, n_seq, n_shard, text_ref, vis_ref, dest_ref, seg_ref, same_ref, pick_ref, slot_ref,
    slot_order_ref, out_ref, kv_buf, aux_buf, vis_stage, vis_buf, key_all, val_all, query_mask, diagonal, slots, live_col,
    send_sem, recv_sem, vis_send, vis_recv,
):
    groups, text, width = text_ref.shape
    query_width = GQ * DH
    rows = out_ref.shape[1]
    slot_count = rows - text
    half = text // 2
    pad = key_all.shape[0] - (REACH + 1) * text
    slot_start = REACH * text + half
    vis_count, vis_block = vis_ref.shape[0], vis_stage.shape[1]
    n_source = n_seq * n_shard
    blocks = n_group * n_seq
    aux_rows = groups * slot_count

    my_group, my_seq, my_shard = lax.axis_index("group"), lax.axis_index("seq"), lax.axis_index("shard")
    here = my_group * n_seq + my_seq
    odd = lax.rem(here, 2)
    upper = lax.rem(here // 2, 2)
    sibling = here + 1 - 2 * odd
    partner = here + 2 - 4 * upper
    me = my_seq * n_shard + my_shard

    def device(block):
        return (block // n_seq, lax.rem(block, n_seq), my_shard)

    def peer(index):
        return (my_group, index // n_shard, lax.rem(index, n_shard))

    barrier = pltpu.get_barrier_semaphore()

    vis_wide = vis_ref[...].astype(jnp.float32)
    dest_wide = dest_ref[...].astype(jnp.float32)
    for shard in range(n_shard):
        listed = [vis_wide[row, shard * groups:(shard + 1) * groups] for row in range(vis_count)]
        names = [jnp.broadcast_to(dest_wide[row:row + 1], (groups, DH)) for row in range(vis_count)]
        if vis_block > vis_count * groups:
            listed.append(jnp.zeros((vis_block - vis_count * groups, width), jnp.float32))
            names.append(jnp.zeros((vis_block - vis_count * groups, DH), jnp.float32))
        vis_stage[shard, :, :width] = jnp.concatenate(listed, axis=0).astype(jnp.bfloat16)
        vis_stage[shard, :, width:] = jnp.concatenate(names, axis=0).astype(jnp.bfloat16)

    def greet(step, carry):
        pl.semaphore_signal(barrier, inc=1, device_id=peer(lax.rem(me + step, n_source)), device_id_type=MESH)
        return carry

    lax.fori_loop(1, n_source, greet, 0)
    pl.semaphore_signal(barrier, inc=1, device_id=device(sibling), device_id_type=MESH)
    pl.semaphore_signal(barrier, inc=1, device_id=device(partner), device_id_type=MESH)

    @pl.when(here >= REACH)
    def _():
        pl.semaphore_signal(barrier, inc=1, device_id=device(here - REACH), device_id_type=MESH)

    for place in range(REACH):
        @pl.when(here < REACH - place)
        def _():
            kv_buf[:, place] = jnp.zeros_like(kv_buf[:, place])
            aux_buf[place] = jnp.zeros_like(aux_buf[place])

    pl.semaphore_wait(barrier, n_source + 1 + (here + REACH < blocks).astype(jnp.int32))

    def landing(item, place):
        return aux_buf.at[place] if item == groups else kv_buf.at[item, place]

    def source(item, place):
        if place < REACH:
            return landing(item, place)
        if item == groups:
            return aux_buf.at[REACH]
        return text_ref.at[item, :, pl.ds(query_width, 2 * DH)]

    def transfer(item, number, place, target_place, target):
        return pltpu.make_async_remote_copy(
            src_ref=source(item, place),
            dst_ref=landing(item, target_place),
            send_sem=send_sem.at[item, number],
            recv_sem=recv_sem.at[item, target_place],
            device_id=device(target),
            device_id_type=MESH,
        )

    own_copies = [
        (here + REACH < blocks, 0, 4, 0, here + REACH),
        (upper == 0, 1, 4, 2, here + 2),
        (odd == 0, 2, 4, 3, here + 1),
    ]
    far_copies = [
        ((here >= 4) & (upper == 1), 3, 0, 2, here - 2),
        ((here >= 4) & (odd == 1), 4, 0, 1, here - 1),
    ]
    near_copies = [
        ((here >= 2) & (odd == 0), 5, 2, 1, here + 1),
        ((here >= 2) & (odd == 1), 5, 2, 3, here - 1),
    ]

    def start(item, copies):
        for condition, number, place, target_place, target in copies:
            @pl.when(condition)
            def _():
                transfer(item, number, place, target_place, target).start()

    def finish(item, copies):
        for condition, number, place, target_place, target in copies:
            @pl.when(condition)
            def _():
                transfer(item, number, place, target_place, target).wait_send()

    def arrive(item, place):
        @pl.when(here >= REACH - place)
        def _():
            transfer(item, 0, place, place, sibling).wait_recv()

    def relay_far(item):
        arrive(item, 0)
        start(item, far_copies)

    def relay_near(item):
        arrive(item, 2)
        start(item, near_copies)

    def vis_copy(step, landing_index):
        target = lax.rem(me + step, n_source)
        return pltpu.make_async_remote_copy(
            src_ref=vis_stage.at[lax.rem(target, n_shard)],
            dst_ref=vis_buf.at[landing_index],
            send_sem=vis_send.at[step],
            recv_sem=vis_recv.at[step],
            device_id=peer(target),
            device_id_type=MESH,
        )

    def vis_start(step, carry):
        vis_copy(step, me).start()
        return carry

    lax.fori_loop(1, n_source, vis_start, 0)
    for item in range(groups):
        start(item, own_copies)
    vis_buf[me] = vis_stage[my_shard]

    def vis_wait(step, carry):
        vis_copy(step, lax.rem(me + n_source - step, n_source)).wait_recv()
        return carry

    lax.fori_loop(1, n_source, vis_wait, 0)

    block_rows = n_shard * vis_block
    my_dest = my_seq.astype(jnp.float32)
    filled = jnp.zeros((aux_rows, 1), jnp.float32)
    for seq in range(n_seq):
        listed = vis_buf[seq * n_shard:(seq + 1) * n_shard].reshape(block_rows, width + DH)
        dest = listed[:, width:].astype(jnp.float32)
        dest_across = dest.T[0:1, :]
        earlier = jnp.where(dest[:, 0:1] == dest_across, same_ref[...], 0.0)
        rank = jnp.sum(earlier, axis=0, keepdims=True)
        placing = jnp.where(
            (slot_ref[...] == rank + float(seq * CAP)) & (dest_across == my_dest), pick_ref[...], 0.0
        )
        part = jnp.dot(placing.astype(jnp.bfloat16), listed[:, :width], preferred_element_type=jnp.float32)
        slots[...] = part if seq == 0 else slots[...] + part
        filled = filled + jnp.sum(placing, axis=1, keepdims=True)
    aux_buf[REACH, 0:aux_rows] = slots[:, query_width:].astype(jnp.bfloat16)
    live_col[...] = jnp.broadcast_to(filled[:slot_count], live_col.shape)
    live_across = live_col[...].T[0:1, :]
    seg_row = seg_ref[...].reshape(1, rows).astype(jnp.float32) + 1.0
    text_tags = seg_row[:, :text]
    slot_tags = jnp.where(live_across > 0, seg_row[:, text:], 0.0)
    tag_rows = jnp.concatenate(
        [
            jnp.broadcast_to(text_tags, (8, text)),
            jnp.concatenate(
                [jnp.broadcast_to(slot_tags, (8, slot_count)), jnp.zeros((8, text - slot_count), jnp.float32)], axis=1
            ),
        ],
        axis=0,
    )
    aux_buf[REACH, aux_rows:] = tag_rows.astype(jnp.bfloat16)
    start(groups, own_copies)

    relay_far(0)
    relay_far(groups)
    relay_near(0)
    relay_near(groups)
    if groups > 1:
        relay_far(1)
    arrive(groups, 1)
    arrive(groups, 3)

    total = key_all.shape[0]
    spare = pad - (REACH + 1) * slot_count
    all_tags = [aux_buf[place, aux_rows:].astype(jnp.float32)[0:1, :] for place in range(REACH)]
    all_tags.append(text_tags[:, :half])
    for place in range(REACH + 1):
        all_tags.append(aux_buf[place, aux_rows:].astype(jnp.float32)[8:9, :slot_count])
    if spare:
        all_tags.append(jnp.zeros((1, spare), jnp.float32))
    all_tags.append(text_tags[:, half:])
    tags = jnp.concatenate(all_tags, axis=1)
    name = lax.broadcasted_iota(jnp.int32, (DH, total), 0)
    at = lax.broadcasted_iota(jnp.int32, (DH, total), 1) - (slot_start + REACH * slot_count)
    differs = (name < OWN) & (name.astype(jnp.float32) + 1.0 != tags)
    own_slot = (name == OWN) & (at >= 0) & (at < slot_count)
    key_all[:, DH:] = jnp.where(differs | own_slot, FAR, 0.0).T.astype(jnp.bfloat16)
    name = lax.broadcasted_iota(jnp.int32, (DH, rows), 0)
    at = lax.broadcasted_iota(jnp.int32, (DH, rows), 1)
    named = (name.astype(jnp.float32) + 1.0 == seg_row) | ((name == OWN) & (at < text))
    query_mask[...] = jnp.where(named, 1.0, 0.0).T.astype(jnp.bfloat16)
    ahead = lax.broadcasted_iota(jnp.int32, (half, half), 0) > lax.broadcasted_iota(jnp.int32, (half, half), 1)
    diagonal[...] = jnp.where(ahead, FAR, 0.0)
    val_all[DH:, :] = jnp.ones_like(val_all[DH:, :])
    scale = LOG2E * DH ** -0.5

    def attend(queries, pieces):
        scores = []
        for low, high, extra in pieces:
            piece = lax.dot_general(
                key_all[low:high], queries, (((1,), (1,)), ((), ())), preferred_element_type=jnp.float32
            )
            scores.append(piece if extra is None else piece + extra)
        largest = functools.reduce(jnp.maximum, [jnp.max(piece, axis=0, keepdims=True) for piece in scores])
        weights = jnp.concatenate(
            [jnp.exp2((piece - largest) * scale).astype(jnp.bfloat16) for piece in scores], axis=0
        )
        summed = jnp.dot(
            val_all[:, pieces[0][0]:pieces[-1][1]], weights, preferred_element_type=jnp.float32
        )
        return (summed[:DH] * (1.0 / summed[DH:DH + 1])).T

    def turned(values):
        return values.astype(jnp.float32).T.astype(jnp.bfloat16)

    slot_end = slot_start + pad
    together = 2
    tiles = (
        (0, ((0, REACH * text, False), (REACH * text, slot_start, True), (slot_start, slot_end, False))),
        (half, ((half, slot_end, False), (slot_end, total, True))),
    )
    for group in range(groups):
        arrive(group, 1)
        arrive(group, 3)
        for place in range(REACH):
            key_all[place * text:(place + 1) * text, :DH] = kv_buf[group, place, :, :DH]
            val_all[:DH, place * text:(place + 1) * text] = turned(kv_buf[group, place, :, DH:])
        own = text_ref[group, :, query_width:]
        key_all[REACH * text:slot_start, :DH] = own[:half, :DH]
        val_all[:DH, REACH * text:slot_start] = turned(own[:half, DH:])
        key_all[slot_end:, :DH] = own[half:, :DH]
        val_all[:DH, slot_end:] = turned(own[half:, DH:])
        slot_rows = [aux_buf[place, group * slot_count:(group + 1) * slot_count] for place in range(REACH + 1)]
        if spare:
            slot_rows.append(jnp.zeros((spare, 2 * DH), jnp.bfloat16))
        slot_rows = jnp.concatenate(slot_rows, axis=0)
        key_all[slot_start:slot_end, :DH] = slot_rows[:, :DH]
        val_all[:DH, slot_start:slot_end] = turned(slot_rows[:, DH:])

        def some_heads(index, carry):
            lanes = [pl.ds(pl.multiple_of((index * together + k) * DH, DH), DH) for k in range(together)]
            wide = jnp.concatenate([diagonal[...]] * together, axis=1)
            for first, pieces in tiles:
                mask = query_mask[first:first + half]
                queries = jnp.concatenate(
                    [
                        jnp.concatenate([text_ref[group, first:first + half, lane], mask], axis=1)
                        for lane in lanes
                    ],
                    axis=0,
                )
                result = attend(
                    queries, [(low, high, wide if last else None) for low, high, last in pieces]
                ).astype(jnp.bfloat16)
                for k, lane in enumerate(lanes):
                    out_ref[group, first:first + half, lane] = result[k * half:(k + 1) * half]
            return carry

        steps = GQ // together
        lax.fori_loop(0, steps // 2, some_heads, 0)
        if group + 1 < groups:
            relay_near(group + 1)
            if group + 2 < groups:
                relay_far(group + 2)
        lax.fori_loop(steps // 2, steps, some_heads, 0)
        slot_queries = slots[group * slot_count:(group + 1) * slot_count, :query_width].astype(jnp.bfloat16)
        mask = query_mask[text:]
        heads = max(1, min(GQ, 256 // slot_count))
        for head in range(0, GQ, heads):
            queries = jnp.concatenate(
                [
                    jnp.concatenate([slot_queries[:, k * DH:(k + 1) * DH], mask], axis=1)
                    for k in range(head, head + heads)
                ],
                axis=0,
            )
            extra = slot_order_ref[:, head * slot_count:(head + heads) * slot_count]
            result = attend(
                queries, [(text, slot_start, None), (slot_start, slot_end, extra), (slot_end, total, None)]
            )
            for k in range(heads):
                kept = jnp.where(live_col[...] > 0, result[k * slot_count:(k + 1) * slot_count], 0.0)
                out_ref[group, text:, (head + k) * DH:(head + k + 1) * DH] = kept.astype(jnp.bfloat16)

    for item in range(groups + 1):
        finish(item, own_copies + far_copies + near_copies)

    def vis_finish(step, carry):
        vis_copy(step, me).wait_send()
        return carry

    lax.fori_loop(1, n_source, vis_finish, 0)


def shards(mesh_shape, text_rows, vis_rows, vis_dest, segments):
    n_group, n_seq, n_shard = (mesh_shape[axis] for axis in ("group", "seq", "shard"))
    text, groups, width = text_rows.shape
    rows = segments.shape[0]
    slot_count = n_seq * CAP
    vis_count = vis_rows.shape[0]
    vis_block = up(vis_count * groups, 16)
    text_t = text_rows.transpose(1, 0, 2)
    index = np.arange(n_shard * vis_block)
    within = index % vis_block
    valid = within < vis_count * groups
    head = within % groups
    same = (head[:, None] == head[None, :]) & (index[:, None] < index[None, :]) & valid[:, None] & valid[None, :]
    place = np.arange(groups * slot_count)
    pick = (place[:, None] // slot_count == head[None, :]) & valid[None, :]
    slot = np.broadcast_to((place % slot_count)[:, None], pick.shape)

    pad = up((REACH + 1) * slot_count, 128)
    own = np.arange(pad) - REACH * slot_count
    behind = (own[:, None] > np.arange(GQ * slot_count)[None, :] % slot_count) & (own < slot_count)[:, None]
    keys = (REACH + 1) * text + pad
    aux_rows = groups * slot_count + 16
    n_source = n_seq * n_shard
    vmem = pl.BlockSpec(memory_space=pltpu.VMEM)
    result = pl.pallas_call(
        functools.partial(kernel, n_group, n_seq, n_shard),
        out_shape=jax.ShapeDtypeStruct((groups, rows, GQ * DH), jnp.bfloat16),
        in_specs=[vmem] * 8,
        out_specs=vmem,
        scratch_shapes=[
            pltpu.VMEM((groups, REACH, text, 2 * DH), jnp.bfloat16),
            pltpu.VMEM((REACH + 1, aux_rows, 2 * DH), jnp.bfloat16),
            pltpu.VMEM((n_shard, vis_block, width + DH), jnp.bfloat16),
            pltpu.VMEM((n_source, vis_block, width + DH), jnp.bfloat16),
            pltpu.VMEM((keys, 2 * DH), jnp.bfloat16),
            pltpu.VMEM((DH + 16, keys), jnp.bfloat16),
            pltpu.VMEM((rows, DH), jnp.bfloat16),
            pltpu.VMEM((text // 2, text // 2), jnp.float32),
            pltpu.VMEM((groups * slot_count, width), jnp.float32),
            pltpu.VMEM((slot_count, DH), jnp.float32),
            pltpu.SemaphoreType.DMA((groups + 1, 6)),
            pltpu.SemaphoreType.DMA((groups + 1, REACH)),
            pltpu.SemaphoreType.DMA((n_source,)),
            pltpu.SemaphoreType.DMA((n_source,)),
        ],
        compiler_params=pltpu.CompilerParams(
            collective_id=0, has_side_effects=True, vmem_limit_bytes=36 * 1024 * 1024
        ),
    )(
        text_t,
        vis_rows,
        jnp.broadcast_to(vis_dest, (vis_count, DH)),
        segments,
        jnp.asarray(same, jnp.float32),
        jnp.asarray(pick, jnp.float32),
        jnp.asarray(slot, jnp.float32),
        jnp.asarray(np.where(behind, FAR, 0.0), jnp.float32),
    )
    return result.transpose(1, 0, 2)


def solution(mesh):
    placed = (
        P(("group", "seq"), "shard", None),
        P(("group", "seq", "shard"), None, None),
        P(("group", "seq", "shard"), None),
        P(("group", "seq")),
    )
    return jax.shard_map(
        functools.partial(shards, dict(mesh.shape)),
        mesh=mesh,
        in_specs=placed,
        out_specs=P(("group", "seq"), "shard", None),
        check_vma=False,
    )
```

```python
import functools
import math

import jax
import jax.numpy as jnp
import numpy as np
from jax import lax
from jax.experimental import pallas as pl
from jax.experimental.pallas import tpu as pltpu
from jax.sharding import PartitionSpec as P

GQ = 8
DH = 128
CAP = 4
REACH = 4
FAR = -(2.0 ** 100)
OWN = 120
LOG2E = math.log2(math.e)
MESH = pl.DeviceIdType.MESH


def up(value, step):
    return -(-value // step) * step


def kernel(
    n_group, n_seq, n_shard, text_ref, vis_ref, dest_ref, seg_ref, same_ref, pick_ref, slot_ref,
    slot_order_ref, out_ref, kv_buf, aux_buf, vis_stage, vis_buf, key_all, val_all, query_mask, diagonal, slots, live_col,
    score_even, score_odd, weight_even, weight_odd,
    send_sem, recv_sem, vis_send, vis_recv,
):
    groups, text, width = text_ref.shape
    query_width = GQ * DH
    rows = out_ref.shape[1]
    slot_count = rows - text
    half = text // 2
    pad = key_all.shape[0] - (REACH + 1) * text
    slot_start = REACH * text + half
    vis_count, vis_block = vis_ref.shape[0], vis_stage.shape[1]
    n_source = n_seq * n_shard
    blocks = n_group * n_seq
    aux_rows = groups * slot_count

    my_group, my_seq, my_shard = lax.axis_index("group"), lax.axis_index("seq"), lax.axis_index("shard")
    here = my_group * n_seq + my_seq
    odd = lax.rem(here, 2)
    upper = lax.rem(here // 2, 2)
    sibling = here + 1 - 2 * odd
    partner = here + 2 - 4 * upper
    me = my_seq * n_shard + my_shard

    def device(block):
        return (block // n_seq, lax.rem(block, n_seq), my_shard)

    def peer(index):
        return (my_group, index // n_shard, lax.rem(index, n_shard))

    barrier = pltpu.get_barrier_semaphore()

    vis_wide = vis_ref[...].astype(jnp.float32)
    dest_wide = dest_ref[...].astype(jnp.float32)
    for shard in range(n_shard):
        listed = [vis_wide[row, shard * groups:(shard + 1) * groups] for row in range(vis_count)]
        names = [jnp.broadcast_to(dest_wide[row:row + 1], (groups, DH)) for row in range(vis_count)]
        if vis_block > vis_count * groups:
            listed.append(jnp.zeros((vis_block - vis_count * groups, width), jnp.float32))
            names.append(jnp.zeros((vis_block - vis_count * groups, DH), jnp.float32))
        vis_stage[shard, :, :width] = jnp.concatenate(listed, axis=0).astype(jnp.bfloat16)
        vis_stage[shard, :, width:] = jnp.concatenate(names, axis=0).astype(jnp.bfloat16)

    def greet(step, carry):
        pl.semaphore_signal(barrier, inc=1, device_id=peer(lax.rem(me + step, n_source)), device_id_type=MESH)
        return carry

    lax.fori_loop(1, n_source, greet, 0)
    pl.semaphore_signal(barrier, inc=1, device_id=device(sibling), device_id_type=MESH)
    pl.semaphore_signal(barrier, inc=1, device_id=device(partner), device_id_type=MESH)

    @pl.when(here >= REACH)
    def _():
        pl.semaphore_signal(barrier, inc=1, device_id=device(here - REACH), device_id_type=MESH)

    for place in range(REACH):
        @pl.when(here < REACH - place)
        def _():
            kv_buf[:, place] = jnp.zeros_like(kv_buf[:, place])
            aux_buf[place] = jnp.zeros_like(aux_buf[place])

    pl.semaphore_wait(barrier, n_source + 1 + (here + REACH < blocks).astype(jnp.int32))

    def is_aux(item):
        return isinstance(item, int) and item == groups

    def landing(item, place):
        return aux_buf.at[place] if is_aux(item) else kv_buf.at[item, place]

    def source(item, place):
        if place < REACH:
            return landing(item, place)
        if is_aux(item):
            return aux_buf.at[REACH]
        return text_ref.at[item, :, pl.ds(query_width, 2 * DH)]

    def transfer(item, number, place, target_place, target):
        return pltpu.make_async_remote_copy(
            src_ref=source(item, place),
            dst_ref=landing(item, target_place),
            send_sem=send_sem.at[item, number],
            recv_sem=recv_sem.at[item, target_place],
            device_id=device(target),
            device_id_type=MESH,
        )

    own_copies = [
        (here + REACH < blocks, 0, 4, 0, here + REACH),
        (upper == 0, 1, 4, 2, here + 2),
        (odd == 0, 2, 4, 3, here + 1),
    ]
    far_copies = [
        ((here >= 4) & (upper == 1), 3, 0, 2, here - 2),
        ((here >= 4) & (odd == 1), 4, 0, 1, here - 1),
    ]
    near_copies = [
        ((here >= 2) & (odd == 0), 5, 2, 1, here + 1),
        ((here >= 2) & (odd == 1), 5, 2, 3, here - 1),
    ]

    def start(item, copies):
        for condition, number, place, target_place, target in copies:
            @pl.when(condition)
            def _():
                transfer(item, number, place, target_place, target).start()

    def finish(item, copies):
        for condition, number, place, target_place, target in copies:
            @pl.when(condition)
            def _():
                transfer(item, number, place, target_place, target).wait_send()

    def arrive(item, place):
        @pl.when(here >= REACH - place)
        def _():
            transfer(item, 0, place, place, sibling).wait_recv()

    def relay_far(item):
        arrive(item, 0)
        start(item, far_copies)

    def relay_near(item):
        arrive(item, 2)
        start(item, near_copies)

    def vis_copy(step, landing_index):
        target = lax.rem(me + step, n_source)
        return pltpu.make_async_remote_copy(
            src_ref=vis_stage.at[lax.rem(target, n_shard)],
            dst_ref=vis_buf.at[landing_index],
            send_sem=vis_send.at[step],
            recv_sem=vis_recv.at[step],
            device_id=peer(target),
            device_id_type=MESH,
        )

    def vis_start(step, carry):
        vis_copy(step, me).start()
        return carry

    lax.fori_loop(1, n_source, vis_start, 0)
    for item in range(groups):
        start(item, own_copies)
    vis_buf[me] = vis_stage[my_shard]

    def vis_wait(step, carry):
        vis_copy(step, lax.rem(me + n_source - step, n_source)).wait_recv()
        return carry

    lax.fori_loop(1, n_source, vis_wait, 0)

    block_rows = n_shard * vis_block
    my_dest = my_seq.astype(jnp.float32)
    filled = jnp.zeros((aux_rows, 1), jnp.float32)
    for seq in range(n_seq):
        listed = vis_buf[seq * n_shard:(seq + 1) * n_shard].reshape(block_rows, width + DH)
        dest = listed[:, width:].astype(jnp.float32)
        dest_across = dest.T[0:1, :]
        earlier = jnp.where(dest[:, 0:1] == dest_across, same_ref[...], 0.0)
        rank = jnp.sum(earlier, axis=0, keepdims=True)
        placing = jnp.where(
            (slot_ref[...] == rank + float(seq * CAP)) & (dest_across == my_dest), pick_ref[...], 0.0
        )
        part = jnp.dot(placing.astype(jnp.bfloat16), listed[:, :width], preferred_element_type=jnp.float32)
        slots[...] = part if seq == 0 else slots[...] + part
        filled = filled + jnp.sum(placing, axis=1, keepdims=True)
    aux_buf[REACH, 0:aux_rows] = slots[:, query_width:].astype(jnp.bfloat16)
    live_col[...] = jnp.broadcast_to(filled[:slot_count], live_col.shape)
    live_across = live_col[...].T[0:1, :]
    seg_row = seg_ref[...].reshape(1, rows).astype(jnp.float32) + 1.0
    text_tags = seg_row[:, :text]
    slot_tags = jnp.where(live_across > 0, seg_row[:, text:], 0.0)
    tag_rows = jnp.concatenate(
        [
            jnp.broadcast_to(text_tags, (8, text)),
            jnp.concatenate(
                [jnp.broadcast_to(slot_tags, (8, slot_count)), jnp.zeros((8, text - slot_count), jnp.float32)], axis=1
            ),
        ],
        axis=0,
    )
    aux_buf[REACH, aux_rows:] = tag_rows.astype(jnp.bfloat16)
    start(groups, own_copies)

    relay_far(0)
    relay_far(groups)
    relay_near(0)
    relay_near(groups)
    if groups > 1:
        relay_far(1)
    arrive(groups, 1)
    arrive(groups, 3)

    total = key_all.shape[0]
    spare = pad - (REACH + 1) * slot_count
    all_tags = [aux_buf[place, aux_rows:].astype(jnp.float32)[0:1, :] for place in range(REACH)]
    all_tags.append(text_tags[:, :half])
    for place in range(REACH + 1):
        all_tags.append(aux_buf[place, aux_rows:].astype(jnp.float32)[8:9, :slot_count])
    if spare:
        all_tags.append(jnp.zeros((1, spare), jnp.float32))
    all_tags.append(text_tags[:, half:])
    tags = jnp.concatenate(all_tags, axis=1)
    name = lax.broadcasted_iota(jnp.int32, (DH, total), 0)
    at = lax.broadcasted_iota(jnp.int32, (DH, total), 1) - (slot_start + REACH * slot_count)
    differs = (name < OWN) & (name.astype(jnp.float32) + 1.0 != tags)
    own_slot = (name == OWN) & (at >= 0) & (at < slot_count)
    key_all[:, DH:] = jnp.where(differs | own_slot, FAR, 0.0).T.astype(jnp.bfloat16)
    name = lax.broadcasted_iota(jnp.int32, (DH, rows), 0)
    at = lax.broadcasted_iota(jnp.int32, (DH, rows), 1)
    named = (name.astype(jnp.float32) + 1.0 == seg_row) | ((name == OWN) & (at < text))
    query_mask[...] = jnp.where(named, 1.0, 0.0).T.astype(jnp.bfloat16)
    ahead = lax.broadcasted_iota(jnp.int32, (half, half), 0) > lax.broadcasted_iota(jnp.int32, (half, half), 1)
    diagonal[...] = jnp.where(ahead, FAR, 0.0)
    val_all[DH:, :] = jnp.ones_like(val_all[DH:, :])
    scale = LOG2E * DH ** -0.5

    def turned(values):
        return values.astype(jnp.float32).T.astype(jnp.bfloat16)

    slot_end = slot_start + pad
    together = 2
    slot_heads = max(1, min(GQ, together * half // slot_count))
    wide = jnp.concatenate([diagonal[...]] * together, axis=1)
    first_pieces = ((0, REACH * text, None), (REACH * text, slot_start, wide), (slot_start, slot_end, None))
    second_pieces = ((half, slot_end, None), (slot_end, total, wide))

    def cut(pieces):
        steps = []
        for low, high, extra in pieces:
            for at in range(low, high, 256):
                end = min(at + 256, high)
                steps.append((at, end, None if extra is None else extra[at - low:end - low]))
        return steps

    def text_tile(group, heads, first, pieces):
        def queries():
            mask = query_mask[first:first + half]
            return jnp.concatenate(
                [
                    jnp.concatenate([text_ref[group, first:first + half, k * DH:(k + 1) * DH], mask], axis=1)
                    for k in heads
                ],
                axis=0,
            )

        def store(result):
            result = result.astype(jnp.bfloat16)
            for number, k in enumerate(heads):
                out_ref[group, first:first + half, k * DH:(k + 1) * DH] = result[number * half:(number + 1) * half]

        return queries, cut(pieces), store

    def slot_tile(group, heads):
        extra = slot_order_ref[:, heads[0] * slot_count:(heads[-1] + 1) * slot_count]
        pieces = ((text, slot_start, None), (slot_start, slot_end, extra), (slot_end, total, None))

        def queries():
            mask = query_mask[text:]
            mine = pl.ds(pl.multiple_of(group * slot_count, slot_count), slot_count)
            rows_of = [slots[mine, k * DH:(k + 1) * DH].astype(jnp.bfloat16) for k in heads]
            return jnp.concatenate([jnp.concatenate([part, mask], axis=1) for part in rows_of], axis=0)

        def store(result):
            for number, k in enumerate(heads):
                kept = jnp.where(live_col[...] > 0, result[number * slot_count:(number + 1) * slot_count], 0.0)
                out_ref[group, text:, k * DH:(k + 1) * DH] = kept.astype(jnp.bfloat16)

        return queries, cut(pieces), store

    score_slots, weight_slots = (score_even, score_odd), (weight_even, weight_odd)

    def one_group(group, carry):
        arrive(group, 1)
        arrive(group, 3)
        for place in range(REACH):
            key_all[place * text:(place + 1) * text, :DH] = kv_buf[group, place, :, :DH]
            val_all[:DH, place * text:(place + 1) * text] = turned(kv_buf[group, place, :, DH:])
        own = text_ref[group, :, query_width:]
        key_all[REACH * text:slot_start, :DH] = own[:half, :DH]
        val_all[:DH, REACH * text:slot_start] = turned(own[:half, DH:])
        key_all[slot_end:, :DH] = own[half:, :DH]
        val_all[:DH, slot_end:] = turned(own[half:, DH:])
        mine = pl.ds(pl.multiple_of(group * slot_count, slot_count), slot_count)
        slot_rows = [aux_buf[place, mine] for place in range(REACH + 1)]
        if spare:
            slot_rows.append(jnp.zeros((spare, 2 * DH), jnp.bfloat16))
        slot_rows = jnp.concatenate(slot_rows, axis=0)
        key_all[slot_start:slot_end, :DH] = slot_rows[:, :DH]
        val_all[:DH, slot_start:slot_end] = turned(slot_rows[:, DH:])

        tiles = []
        for head in range(0, GQ, together):
            heads = range(head, head + together)
            tiles.append(text_tile(group, heads, 0, first_pieces))
            tiles.append(text_tile(group, heads, half, second_pieces))
        for head in range(0, GQ, slot_heads):
            tiles.append(slot_tile(group, range(head, head + slot_heads)))

        def score_steps(number):
            queries, steps, _ = tiles[number]
            held = score_slots[number % 2]
            state = {"queries": queries(), "largest": None}

            def one(step):
                low, high, extra = step
                piece = lax.dot_general(
                    key_all[low:high], state["queries"], (((1,), (1,)), ((), ())),
                    preferred_element_type=jnp.float32,
                )
                if extra is not None:
                    piece = piece + extra
                at, lanes = low - steps[0][0], piece.shape[1]
                held[at:at + high - low, :lanes] = piece
                part = jnp.max(piece.reshape((high - low) // 8, 8, lanes), axis=0)
                state["largest"] = part if state["largest"] is None else jnp.maximum(state["largest"], part)

            return [functools.partial(one, step) for step in steps], state

        def weight_steps(number, state):
            steps = tiles[number][1]
            held, made = score_slots[number % 2], weight_slots[number % 2]
            lanes = state["largest"].shape[1]
            largest = jnp.max(state["largest"], axis=0, keepdims=True)

            def one(at, end):
                made[at:end, :lanes] = jnp.exp2((held[at:end, :lanes] - largest) * scale).astype(jnp.bfloat16)

            count = steps[-1][1] - steps[0][0]
            return [functools.partial(one, at, min(at + 64, count)) for at in range(0, count, 64)], lanes

        def finish_tile(number, lanes):
            _, steps, store = tiles[number]
            low, high = steps[0][0], steps[-1][1]
            summed = jnp.dot(
                val_all[:, low:high], weight_slots[number % 2][:high - low, :lanes],
                preferred_element_type=jnp.float32,
            )
            store((summed[:DH] * (1.0 / summed[DH:DH + 1])).T)

        work, state = score_steps(0)
        for step in work:
            step()
        before = None
        for number in range(len(tiles)):
            if number == len(tiles) // 2:
                @pl.when(group + 1 < groups)
                def _():
                    relay_near(group + 1)

                @pl.when(group + 2 < groups)
                def _():
                    relay_far(group + 2)
            if before is not None:
                finish_tile(number - 1, before)
            weigh, lanes = weight_steps(number, state)
            score = []
            if number + 1 < len(tiles):
                score, state = score_steps(number + 1)
            done = 0
            for position, step in enumerate(score):
                step()
                until = (position + 1) * len(weigh) // len(score)
                for part in weigh[done:until]:
                    part()
                done = until
            for part in weigh[done:]:
                part()
            before = lanes
        finish_tile(len(tiles) - 1, before)
        return carry

    lax.fori_loop(0, groups, one_group, 0)

    for item in range(groups + 1):
        finish(item, own_copies + far_copies + near_copies)

    def vis_finish(step, carry):
        vis_copy(step, me).wait_send()
        return carry

    lax.fori_loop(1, n_source, vis_finish, 0)


def shards(mesh_shape, text_rows, vis_rows, vis_dest, segments):
    n_group, n_seq, n_shard = (mesh_shape[axis] for axis in ("group", "seq", "shard"))
    text, groups, width = text_rows.shape
    rows = segments.shape[0]
    slot_count = n_seq * CAP
    vis_count = vis_rows.shape[0]
    vis_block = up(vis_count * groups, 16)
    text_t = text_rows.transpose(1, 0, 2)
    index = np.arange(n_shard * vis_block)
    within = index % vis_block
    valid = within < vis_count * groups
    head = within % groups
    same = (head[:, None] == head[None, :]) & (index[:, None] < index[None, :]) & valid[:, None] & valid[None, :]
    place = np.arange(groups * slot_count)
    pick = (place[:, None] // slot_count == head[None, :]) & valid[None, :]
    slot = np.broadcast_to((place % slot_count)[:, None], pick.shape)

    pad = up((REACH + 1) * slot_count, 128)
    own = np.arange(pad) - REACH * slot_count
    behind = (own[:, None] > np.arange(GQ * slot_count)[None, :] % slot_count) & (own < slot_count)[:, None]
    keys = (REACH + 1) * text + pad
    aux_rows = groups * slot_count + 16
    n_source = n_seq * n_shard
    vmem = pl.BlockSpec(memory_space=pltpu.VMEM)
    result = pl.pallas_call(
        functools.partial(kernel, n_group, n_seq, n_shard),
        out_shape=jax.ShapeDtypeStruct((groups, rows, GQ * DH), jnp.bfloat16),
        in_specs=[vmem] * 8,
        out_specs=vmem,
        scratch_shapes=[
            pltpu.VMEM((groups, REACH, text, 2 * DH), jnp.bfloat16),
            pltpu.VMEM((REACH + 1, aux_rows, 2 * DH), jnp.bfloat16),
            pltpu.VMEM((n_shard, vis_block, width + DH), jnp.bfloat16),
            pltpu.VMEM((n_source, vis_block, width + DH), jnp.bfloat16),
            pltpu.VMEM((keys, 2 * DH), jnp.bfloat16),
            pltpu.VMEM((DH + 16, keys), jnp.bfloat16),
            pltpu.VMEM((rows, DH), jnp.bfloat16),
            pltpu.VMEM((text // 2, text // 2), jnp.float32),
            pltpu.VMEM((groups * slot_count, width), jnp.float32),
            pltpu.VMEM((slot_count, DH), jnp.float32),
            pltpu.VMEM((keys - text // 2, text), jnp.float32),
            pltpu.VMEM((keys - text // 2, text), jnp.float32),
            pltpu.VMEM((keys - text // 2, text), jnp.bfloat16),
            pltpu.VMEM((keys - text // 2, text), jnp.bfloat16),
            pltpu.SemaphoreType.DMA((groups + 1, 6)),
            pltpu.SemaphoreType.DMA((groups + 1, REACH)),
            pltpu.SemaphoreType.DMA((n_source,)),
            pltpu.SemaphoreType.DMA((n_source,)),
        ],
        compiler_params=pltpu.CompilerParams(
            collective_id=0, has_side_effects=True, vmem_limit_bytes=36 * 1024 * 1024
        ),
    )(
        text_t,
        vis_rows,
        jnp.broadcast_to(vis_dest, (vis_count, DH)),
        segments,
        jnp.asarray(same, jnp.float32),
        jnp.asarray(pick, jnp.float32),
        jnp.asarray(slot, jnp.float32),
        jnp.asarray(np.where(behind, FAR, 0.0), jnp.float32),
    )
    return result.transpose(1, 0, 2)


def solution(mesh):
    placed = (
        P(("group", "seq"), "shard", None),
        P(("group", "seq", "shard"), None, None),
        P(("group", "seq", "shard"), None),
        P(("group", "seq")),
    )
    return jax.shard_map(
        functools.partial(shards, dict(mesh.shape)),
        mesh=mesh,
        in_specs=placed,
        out_specs=P(("group", "seq"), "shard", None),
        check_vma=False,
    )
```

```python
import functools
import math

import jax
import jax.numpy as jnp
import numpy as np
from jax import lax
from jax.experimental import pallas as pl
from jax.experimental.pallas import tpu as pltpu
from jax.sharding import PartitionSpec as P

GQ = 8
DH = 128
CAP = 4
REACH = 4
FAR = -(2.0 ** 100)
OWN = 120
LOG2E = math.log2(math.e)
MESH = pl.DeviceIdType.MESH


def up(value, step):
    return -(-value // step) * step


def kernel(
    n_group, n_seq, n_shard, text_ref, vis_ref, dest_ref, seg_ref, same_ref, pick_ref, slot_ref,
    slot_order_ref, out_ref, kv_buf, aux_buf, key_stage, key_listed, query_stage, query_listed, placed, key_all, val_all,
    text_mask, slot_mask, diagonal, slots, live_col,
    score_even, score_odd, weight_even, weight_odd,
    send_sem, recv_sem, key_send, key_recv, query_send, query_recv,
):
    groups, text, width = text_ref.shape
    query_width = GQ * DH
    rows = out_ref.shape[1]
    slot_count = rows - text
    half = text // 2
    pad = key_all.shape[0] - (REACH + 1) * text
    slot_start = REACH * text + half
    vis_count, vis_block = vis_ref.shape[0], key_stage.shape[1]
    n_source = n_seq * n_shard
    blocks = n_group * n_seq
    aux_rows = groups * slot_count

    my_group, my_seq, my_shard = lax.axis_index("group"), lax.axis_index("seq"), lax.axis_index("shard")
    here = my_group * n_seq + my_seq
    odd = lax.rem(here, 2)
    upper = lax.rem(here // 2, 2)
    sibling = here + 1 - 2 * odd
    partner = here + 2 - 4 * upper
    me = my_seq * n_shard + my_shard

    def device(block):
        return (block // n_seq, lax.rem(block, n_seq), my_shard)

    def peer(index):
        return (my_group, index // n_shard, lax.rem(index, n_shard))

    barrier = pltpu.get_barrier_semaphore()

    vis_wide = vis_ref[...].astype(jnp.float32)
    dest_wide = dest_ref[...].astype(jnp.float32)
    for shard in range(n_shard):
        listed = [vis_wide[row, shard * groups:(shard + 1) * groups] for row in range(vis_count)]
        names = [jnp.broadcast_to(dest_wide[row:row + 1], (groups, DH)) for row in range(vis_count)]
        if vis_block > vis_count * groups:
            listed.append(jnp.zeros((vis_block - vis_count * groups, width), jnp.float32))
            names.append(jnp.zeros((vis_block - vis_count * groups, DH), jnp.float32))
        listed = jnp.concatenate(listed, axis=0).astype(jnp.bfloat16)
        query_stage[shard] = listed[:, :query_width]
        key_stage[shard, :, :2 * DH] = listed[:, query_width:]
        key_stage[shard, :, 2 * DH:] = jnp.concatenate(names, axis=0).astype(jnp.bfloat16)

    def greet(step, carry):
        pl.semaphore_signal(barrier, inc=1, device_id=peer(lax.rem(me + step, n_source)), device_id_type=MESH)
        return carry

    lax.fori_loop(1, n_source, greet, 0)
    pl.semaphore_signal(barrier, inc=1, device_id=device(sibling), device_id_type=MESH)
    pl.semaphore_signal(barrier, inc=1, device_id=device(partner), device_id_type=MESH)

    @pl.when(here >= REACH)
    def _():
        pl.semaphore_signal(barrier, inc=1, device_id=device(here - REACH), device_id_type=MESH)

    for place in range(REACH):
        @pl.when(here < REACH - place)
        def _():
            kv_buf[:, place] = jnp.zeros_like(kv_buf[:, place])
            aux_buf[place] = jnp.zeros_like(aux_buf[place])

    pl.semaphore_wait(barrier, n_source + 1 + (here + REACH < blocks).astype(jnp.int32))

    def is_aux(item):
        return isinstance(item, int) and item == groups

    def landing(item, place):
        return aux_buf.at[place] if is_aux(item) else kv_buf.at[item, place]

    def source(item, place):
        if place < REACH:
            return landing(item, place)
        if is_aux(item):
            return aux_buf.at[REACH]
        return text_ref.at[item, :, pl.ds(query_width, 2 * DH)]

    def transfer(item, number, place, target_place, target):
        return pltpu.make_async_remote_copy(
            src_ref=source(item, place),
            dst_ref=landing(item, target_place),
            send_sem=send_sem.at[item, number],
            recv_sem=recv_sem.at[item, target_place],
            device_id=device(target),
            device_id_type=MESH,
        )

    own_copies = [
        (here + REACH < blocks, 0, 4, 0, here + REACH),
        (upper == 0, 1, 4, 2, here + 2),
        (odd == 0, 2, 4, 3, here + 1),
    ]
    far_copies = [
        ((here >= 4) & (upper == 1), 3, 0, 2, here - 2),
        ((here >= 4) & (odd == 1), 4, 0, 1, here - 1),
    ]
    near_copies = [
        ((here >= 2) & (odd == 0), 5, 2, 1, here + 1),
        ((here >= 2) & (odd == 1), 5, 2, 3, here - 1),
    ]

    def start(item, copies):
        for condition, number, place, target_place, target in copies:
            @pl.when(condition)
            def _():
                transfer(item, number, place, target_place, target).start()

    def finish(item, copies):
        for condition, number, place, target_place, target in copies:
            @pl.when(condition)
            def _():
                transfer(item, number, place, target_place, target).wait_send()

    def arrive(item, place):
        @pl.when(here >= REACH - place)
        def _():
            transfer(item, 0, place, place, sibling).wait_recv()

    def relay_far(item):
        arrive(item, 0)
        start(item, far_copies)

    def relay_near(item):
        arrive(item, 2)
        start(item, near_copies)

    def vis_copy(parts, step, landing_index):
        stage, listed, sent, received = parts
        target = lax.rem(me + step, n_source)
        return pltpu.make_async_remote_copy(
            src_ref=stage.at[lax.rem(target, n_shard)],
            dst_ref=listed.at[landing_index],
            send_sem=sent.at[step],
            recv_sem=received.at[step],
            device_id=peer(target),
            device_id_type=MESH,
        )

    def vis_start(parts):
        def one(step, carry):
            vis_copy(parts, step, me).start()
            return carry

        lax.fori_loop(1, n_source, one, 0)
        parts[1][me] = parts[0][my_shard]

    def vis_wait(parts):
        def one(step, carry):
            vis_copy(parts, step, lax.rem(me + n_source - step, n_source)).wait_recv()
            return carry

        lax.fori_loop(1, n_source, one, 0)

    def vis_finish(parts):
        def one(step, carry):
            vis_copy(parts, step, me).wait_send()
            return carry

        lax.fori_loop(1, n_source, one, 0)

    key_parts = (key_stage, key_listed, key_send, key_recv)
    query_parts = (query_stage, query_listed, query_send, query_recv)
    vis_start(key_parts)
    start(0, own_copies)
    vis_wait(key_parts)

    block_rows = n_shard * vis_block
    my_dest = my_seq.astype(jnp.float32)
    filled = jnp.zeros((aux_rows, 1), jnp.float32)
    for seq in range(n_seq):
        listed = key_listed[seq * n_shard:(seq + 1) * n_shard].reshape(block_rows, 3 * DH)
        dest = listed[:, 2 * DH:].astype(jnp.float32)
        dest_across = dest.T[0:1, :]
        earlier = jnp.where(dest[:, 0:1] == dest_across, same_ref[...], 0.0)
        rank = jnp.sum(earlier, axis=0, keepdims=True)
        placing = jnp.where(
            (slot_ref[...] == rank + float(seq * CAP)) & (dest_across == my_dest), pick_ref[...], 0.0
        )
        placing = placing.astype(jnp.bfloat16)
        placed[:, seq * block_rows:(seq + 1) * block_rows] = placing
        part = jnp.dot(placing, listed[:, :2 * DH], preferred_element_type=jnp.float32)
        slot_keys = part if seq == 0 else slot_keys + part
        filled = filled + jnp.sum(placing.astype(jnp.float32), axis=1, keepdims=True)
    aux_buf[REACH, 0:aux_rows] = slot_keys.astype(jnp.bfloat16)
    live_col[...] = jnp.broadcast_to(filled[:slot_count], live_col.shape)
    live_across = live_col[...].T[0:1, :]
    seg_row = seg_ref[...].reshape(1, rows).astype(jnp.float32) + 1.0
    text_tags = seg_row[:, :text]
    slot_tags = jnp.where(live_across > 0, seg_row[:, text:], 0.0)
    tag_rows = jnp.concatenate(
        [
            jnp.broadcast_to(text_tags, (8, text)),
            jnp.concatenate(
                [jnp.broadcast_to(slot_tags, (8, slot_count)), jnp.zeros((8, text - slot_count), jnp.float32)], axis=1
            ),
        ],
        axis=0,
    )
    aux_buf[REACH, aux_rows:] = tag_rows.astype(jnp.bfloat16)
    start(groups, own_copies)
    vis_start(query_parts)
    for item in range(1, groups):
        start(item, own_copies)

    relay_far(0)
    relay_far(groups)
    relay_near(0)
    relay_near(groups)
    if groups > 1:
        relay_far(1)
    arrive(groups, 1)
    arrive(groups, 3)

    total = key_all.shape[0]
    spare = pad - (REACH + 1) * slot_count
    all_tags = [aux_buf[place, aux_rows:].astype(jnp.float32)[0:1, :] for place in range(REACH)]
    all_tags.append(text_tags[:, :half])
    for place in range(REACH + 1):
        all_tags.append(aux_buf[place, aux_rows:].astype(jnp.float32)[8:9, :slot_count])
    if spare:
        all_tags.append(jnp.zeros((1, spare), jnp.float32))
    all_tags.append(text_tags[:, half:])
    tags = jnp.concatenate(all_tags, axis=1)
    name = lax.broadcasted_iota(jnp.int32, (DH, total), 0)
    at = lax.broadcasted_iota(jnp.int32, (DH, total), 1) - (slot_start + REACH * slot_count)
    differs = (name < OWN) & (name.astype(jnp.float32) + 1.0 != tags)
    own_slot = (name == OWN) & (at >= 0) & (at < slot_count)
    key_all[:, DH:] = jnp.where(differs | own_slot, FAR, 0.0).T.astype(jnp.bfloat16)
    together = 2
    slot_heads = max(1, min(GQ, together * half // slot_count))
    name = lax.broadcasted_iota(jnp.int32, (DH, rows), 0)
    at = lax.broadcasted_iota(jnp.int32, (DH, rows), 1)
    named = jnp.where((name.astype(jnp.float32) + 1.0 == seg_row) | ((name == OWN) & (at < text)), 1.0, 0.0)
    for part in range(2):
        narrow = named[:, part * half:(part + 1) * half].astype(jnp.bfloat16)
        text_mask[part] = jnp.concatenate([narrow] * together, axis=1)
    slot_mask[...] = jnp.concatenate([named[:, text:]] * slot_heads, axis=1).astype(jnp.bfloat16)
    ahead = lax.broadcasted_iota(jnp.int32, (half, half), 0) > lax.broadcasted_iota(jnp.int32, (half, half), 1)
    diagonal[...] = jnp.where(ahead, FAR, 0.0)
    val_all[DH:, :] = jnp.ones_like(val_all[DH:, :])
    scale = LOG2E * DH ** -0.5

    def turned(values):
        return values.astype(jnp.float32).T.astype(jnp.bfloat16)

    slot_end = slot_start + pad
    wide = jnp.concatenate([diagonal[...]] * together, axis=1)
    first_span = (0, slot_end, REACH * text, slot_start, wide)
    second_span = (half, total, slot_end, total, wide)

    def text_tile(group, heads, part, span):
        mine = slice(part * half, (part + 1) * half)

        def queries():
            rows_of = [text_ref[group, mine, k * DH:(k + 1) * DH] for k in heads]
            return jnp.concatenate([turned(jnp.concatenate(rows_of, axis=0)), text_mask[part]], axis=0)

        def store(result):
            result = result.astype(jnp.bfloat16)
            for number, k in enumerate(heads):
                out_ref[group, mine, k * DH:(k + 1) * DH] = result[number * half:(number + 1) * half]

        return queries, span, store

    def slot_tile(group, heads):
        extra = slot_order_ref[:, heads[0] * slot_count:(heads[-1] + 1) * slot_count]

        def queries():
            mine = pl.ds(pl.multiple_of(group * slot_count, slot_count), slot_count)
            rows_of = [slots[mine, k * DH:(k + 1) * DH] for k in heads]
            return jnp.concatenate([turned(jnp.concatenate(rows_of, axis=0)), slot_mask[...]], axis=0)

        def store(result):
            for number, k in enumerate(heads):
                kept = jnp.where(live_col[...] > 0, result[number * slot_count:(number + 1) * slot_count], 0.0)
                out_ref[group, text:, k * DH:(k + 1) * DH] = kept.astype(jnp.bfloat16)

        return queries, (text, total, slot_start, slot_end, extra), store

    vis_wait(query_parts)
    slots[...] = jnp.dot(
        placed[...], query_listed[...].reshape(n_source * vis_block, query_width), preferred_element_type=jnp.float32
    )
    score_slots, weight_slots = (score_even, score_odd), (weight_even, weight_odd)

    def one_group(group, carry):
        arrive(group, 1)
        arrive(group, 3)
        for place in range(REACH):
            key_all[place * text:(place + 1) * text, :DH] = kv_buf[group, place, :, :DH]
            val_all[:DH, place * text:(place + 1) * text] = turned(kv_buf[group, place, :, DH:])
        own = text_ref[group, :, query_width:]
        key_all[REACH * text:slot_start, :DH] = own[:half, :DH]
        val_all[:DH, REACH * text:slot_start] = turned(own[:half, DH:])
        key_all[slot_end:, :DH] = own[half:, :DH]
        val_all[:DH, slot_end:] = turned(own[half:, DH:])
        mine = pl.ds(pl.multiple_of(group * slot_count, slot_count), slot_count)
        slot_rows = [aux_buf[place, mine] for place in range(REACH + 1)]
        if spare:
            slot_rows.append(jnp.zeros((spare, 2 * DH), jnp.bfloat16))
        slot_rows = jnp.concatenate(slot_rows, axis=0)
        key_all[slot_start:slot_end, :DH] = slot_rows[:, :DH]
        val_all[:DH, slot_start:slot_end] = turned(slot_rows[:, DH:])

        tiles = []
        for head in range(0, GQ, together):
            heads = range(head, head + together)
            tiles.append(text_tile(group, heads, 0, first_span))
            tiles.append(text_tile(group, heads, 1, second_span))
        for head in range(0, GQ, slot_heads):
            tiles.append(slot_tile(group, range(head, head + slot_heads)))

        def score_steps(number):
            queries, (low, high, extra_low, extra_high, extra), _ = tiles[number]
            held = score_slots[number % 2]
            state = {"queries": queries(), "largest": None}

            def one(start_at, end_at):
                result = jnp.dot(key_all[start_at:end_at], state["queries"], preferred_element_type=jnp.float32)
                lanes = result.shape[1]
                for at in range(start_at, end_at, 128):
                    piece = result[at - start_at:at - start_at + 128]
                    if extra_low <= at < extra_high:
                        piece = piece + extra[at - extra_low:at - extra_low + 128]
                    held[at - low:at - low + 128, :lanes] = piece
                    part = jnp.max(piece.reshape(16, 8, lanes), axis=0)
                    state["largest"] = part if state["largest"] is None else jnp.maximum(state["largest"], part)

            middle = low + (high - low) // 256 * 128
            return [functools.partial(one, low, middle), functools.partial(one, middle, high)], state

        def weight_steps(number, state):
            low, high = tiles[number][1][:2]
            held, made = score_slots[number % 2], weight_slots[number % 2]
            lanes = state["largest"].shape[1]
            largest = jnp.max(state["largest"], axis=0, keepdims=True)

            def one(at, end):
                made[at:end, :lanes] = jnp.exp2((held[at:end, :lanes] - largest) * scale).astype(jnp.bfloat16)

            count = high - low
            return [functools.partial(one, at, min(at + 64, count)) for at in range(0, count, 64)], lanes

        def finish_tile(number, lanes):
            _, (low, high, *_), store = tiles[number]
            summed = jnp.dot(
                val_all[:, low:high], weight_slots[number % 2][:high - low, :lanes],
                preferred_element_type=jnp.float32,
            )
            store((summed[:DH] * (1.0 / summed[DH:DH + 1])).T)

        work, state = score_steps(0)
        for step in work:
            step()
        before = None
        for number in range(len(tiles)):
            if number == len(tiles) // 2:
                @pl.when(group + 1 < groups)
                def _():
                    relay_near(group + 1)

                @pl.when(group + 2 < groups)
                def _():
                    relay_far(group + 2)
            if before is not None:
                finish_tile(number - 1, before)
            weigh, lanes = weight_steps(number, state)
            score = []
            if number + 1 < len(tiles):
                score, state = score_steps(number + 1)
            done = 0
            for position, step in enumerate(score):
                step()
                until = (position + 1) * len(weigh) // len(score)
                for part in weigh[done:until]:
                    part()
                done = until
            for part in weigh[done:]:
                part()
            before = lanes
        finish_tile(len(tiles) - 1, before)
        return carry

    lax.fori_loop(0, groups, one_group, 0)

    for item in range(groups + 1):
        finish(item, own_copies + far_copies + near_copies)

    vis_finish(key_parts)
    vis_finish(query_parts)


def shards(mesh_shape, text_rows, vis_rows, vis_dest, segments):
    n_group, n_seq, n_shard = (mesh_shape[axis] for axis in ("group", "seq", "shard"))
    text, groups, width = text_rows.shape
    rows = segments.shape[0]
    slot_count = n_seq * CAP
    vis_count = vis_rows.shape[0]
    vis_block = up(vis_count * groups, 16)
    text_t = text_rows.transpose(1, 0, 2)
    index = np.arange(n_shard * vis_block)
    within = index % vis_block
    valid = within < vis_count * groups
    head = within % groups
    same = (head[:, None] == head[None, :]) & (index[:, None] < index[None, :]) & valid[:, None] & valid[None, :]
    place = np.arange(groups * slot_count)
    pick = (place[:, None] // slot_count == head[None, :]) & valid[None, :]
    slot = np.broadcast_to((place % slot_count)[:, None], pick.shape)

    pad = up((REACH + 1) * slot_count, 128)
    own = np.arange(pad) - REACH * slot_count
    behind = (own[:, None] > np.arange(GQ * slot_count)[None, :] % slot_count) & (own < slot_count)[:, None]
    keys = (REACH + 1) * text + pad
    aux_rows = groups * slot_count + 16
    n_source = n_seq * n_shard
    vmem = pl.BlockSpec(memory_space=pltpu.VMEM)
    result = pl.pallas_call(
        functools.partial(kernel, n_group, n_seq, n_shard),
        out_shape=jax.ShapeDtypeStruct((groups, rows, GQ * DH), jnp.bfloat16),
        in_specs=[vmem] * 8,
        out_specs=vmem,
        scratch_shapes=[
            pltpu.VMEM((groups, REACH, text, 2 * DH), jnp.bfloat16),
            pltpu.VMEM((REACH + 1, aux_rows, 2 * DH), jnp.bfloat16),
            pltpu.VMEM((n_shard, vis_block, 3 * DH), jnp.bfloat16),
            pltpu.VMEM((n_source, vis_block, 3 * DH), jnp.bfloat16),
            pltpu.VMEM((n_shard, vis_block, GQ * DH), jnp.bfloat16),
            pltpu.VMEM((n_source, vis_block, GQ * DH), jnp.bfloat16),
            pltpu.VMEM((groups * slot_count, n_source * vis_block), jnp.bfloat16),
            pltpu.VMEM((keys, 2 * DH), jnp.bfloat16),
            pltpu.VMEM((DH + 16, keys), jnp.bfloat16),
            pltpu.VMEM((2, DH, text), jnp.bfloat16),
            pltpu.VMEM((DH, min(GQ * slot_count, text)), jnp.bfloat16),
            pltpu.VMEM((text // 2, text // 2), jnp.float32),
            pltpu.VMEM((groups * slot_count, GQ * DH), jnp.float32),
            pltpu.VMEM((slot_count, DH), jnp.float32),
            pltpu.VMEM((keys - text // 2, text), jnp.float32),
            pltpu.VMEM((keys - text // 2, text), jnp.float32),
            pltpu.VMEM((keys - text // 2, text), jnp.bfloat16),
            pltpu.VMEM((keys - text // 2, text), jnp.bfloat16),
            pltpu.SemaphoreType.DMA((groups + 1, 6)),
            pltpu.SemaphoreType.DMA((groups + 1, REACH)),
            pltpu.SemaphoreType.DMA((n_source,)),
            pltpu.SemaphoreType.DMA((n_source,)),
            pltpu.SemaphoreType.DMA((n_source,)),
            pltpu.SemaphoreType.DMA((n_source,)),
        ],
        compiler_params=pltpu.CompilerParams(
            collective_id=0, has_side_effects=True, vmem_limit_bytes=36 * 1024 * 1024
        ),
    )(
        text_t,
        vis_rows,
        jnp.broadcast_to(vis_dest, (vis_count, DH)),
        segments,
        jnp.asarray(same, jnp.float32),
        jnp.asarray(pick, jnp.float32),
        jnp.asarray(slot, jnp.float32),
        jnp.asarray(np.where(behind, FAR, 0.0), jnp.float32),
    )
    return result.transpose(1, 0, 2)


def solution(mesh):
    placed = (
        P(("group", "seq"), "shard", None),
        P(("group", "seq", "shard"), None, None),
        P(("group", "seq", "shard"), None),
        P(("group", "seq")),
    )
    return jax.shard_map(
        functools.partial(shards, dict(mesh.shape)),
        mesh=mesh,
        in_specs=placed,
        out_specs=P(("group", "seq"), "shard", None),
        check_vma=False,
    )
```

```python
import functools
import math

import jax
import jax.numpy as jnp
import numpy as np
from jax import lax
from jax.experimental import pallas as pl
from jax.experimental.pallas import tpu as pltpu
from jax.sharding import PartitionSpec as P

GQ = 8
DH = 128
CAP = 4
REACH = 4
FAR = -(2.0 ** 100)
OWN = 120
TOGETHER = 4
LOG2E = math.log2(math.e)
MESH = pl.DeviceIdType.MESH


def up(value, step):
    return -(-value // step) * step


def kernel(
    n_group, n_seq, n_shard, text_ref, vis_ref, dest_ref, seg_ref, same_ref, pick_ref, slot_ref,
    slot_order_ref, out_ref, kv_buf, aux_buf, key_stage, key_listed, query_stage, query_listed, placed, key_all, val_all,
    text_mask, slot_mask, diagonal, slots, live_col,
    score_even, score_odd, weight_even, weight_odd,
    send_sem, recv_sem, key_send, key_recv, query_send, query_recv,
):
    groups, text, width = text_ref.shape
    query_width = GQ * DH
    rows = out_ref.shape[1]
    slot_count = rows - text
    half = text // 2
    pad = key_all.shape[0] - (REACH + 1) * text
    slot_start = REACH * text + half
    vis_count, vis_block = vis_ref.shape[0], key_stage.shape[1]
    n_source = n_seq * n_shard
    blocks = n_group * n_seq
    aux_rows = groups * slot_count

    my_group, my_seq, my_shard = lax.axis_index("group"), lax.axis_index("seq"), lax.axis_index("shard")
    here = my_group * n_seq + my_seq
    odd = lax.rem(here, 2)
    upper = lax.rem(here // 2, 2)
    sibling = here + 1 - 2 * odd
    partner = here + 2 - 4 * upper
    me = my_seq * n_shard + my_shard

    def device(block):
        return (block // n_seq, lax.rem(block, n_seq), my_shard)

    def peer(index):
        return (my_group, index // n_shard, lax.rem(index, n_shard))

    barrier = pltpu.get_barrier_semaphore()

    vis_wide = vis_ref[...].astype(jnp.float32)
    dest_wide = dest_ref[...].astype(jnp.float32)
    for shard in range(n_shard):
        listed = [vis_wide[row, shard * groups:(shard + 1) * groups] for row in range(vis_count)]
        names = [jnp.broadcast_to(dest_wide[row:row + 1], (groups, DH)) for row in range(vis_count)]
        if vis_block > vis_count * groups:
            listed.append(jnp.zeros((vis_block - vis_count * groups, width), jnp.float32))
            names.append(jnp.zeros((vis_block - vis_count * groups, DH), jnp.float32))
        listed = jnp.concatenate(listed, axis=0).astype(jnp.bfloat16)
        query_stage[shard] = listed[:, :query_width]
        key_stage[shard, :, :2 * DH] = listed[:, query_width:]
        key_stage[shard, :, 2 * DH:] = jnp.concatenate(names, axis=0).astype(jnp.bfloat16)

    def greet(step, carry):
        pl.semaphore_signal(barrier, inc=1, device_id=peer(lax.rem(me + step, n_source)), device_id_type=MESH)
        return carry

    lax.fori_loop(1, n_source, greet, 0)
    pl.semaphore_signal(barrier, inc=1, device_id=device(sibling), device_id_type=MESH)
    pl.semaphore_signal(barrier, inc=1, device_id=device(partner), device_id_type=MESH)

    @pl.when(here >= REACH)
    def _():
        pl.semaphore_signal(barrier, inc=1, device_id=device(here - REACH), device_id_type=MESH)

    for place in range(REACH):
        @pl.when(here < REACH - place)
        def _():
            kv_buf[:, place] = jnp.zeros_like(kv_buf[:, place])
            aux_buf[place] = jnp.zeros_like(aux_buf[place])

    pl.semaphore_wait(barrier, n_source + 1 + (here + REACH < blocks).astype(jnp.int32))

    def is_aux(item):
        return isinstance(item, int) and item == groups

    def landing(item, place):
        return aux_buf.at[place] if is_aux(item) else kv_buf.at[item, place]

    def source(item, place):
        if place < REACH:
            return landing(item, place)
        if is_aux(item):
            return aux_buf.at[REACH]
        return text_ref.at[item, :, pl.ds(query_width, 2 * DH)]

    def transfer(item, number, place, target_place, target):
        return pltpu.make_async_remote_copy(
            src_ref=source(item, place),
            dst_ref=landing(item, target_place),
            send_sem=send_sem.at[item, number],
            recv_sem=recv_sem.at[item, target_place],
            device_id=device(target),
            device_id_type=MESH,
        )

    own_copies = [
        (here + REACH < blocks, 0, 4, 0, here + REACH),
        (upper == 0, 1, 4, 2, here + 2),
        (odd == 0, 2, 4, 3, here + 1),
    ]
    far_copies = [
        ((here >= 4) & (upper == 1), 3, 0, 2, here - 2),
        ((here >= 4) & (odd == 1), 4, 0, 1, here - 1),
    ]
    near_copies = [
        ((here >= 2) & (odd == 0), 5, 2, 1, here + 1),
        ((here >= 2) & (odd == 1), 5, 2, 3, here - 1),
    ]

    def start(item, copies):
        for condition, number, place, target_place, target in copies:
            @pl.when(condition)
            def _():
                transfer(item, number, place, target_place, target).start()

    def finish(item, copies):
        for condition, number, place, target_place, target in copies:
            @pl.when(condition)
            def _():
                transfer(item, number, place, target_place, target).wait_send()

    def arrive(item, place):
        @pl.when(here >= REACH - place)
        def _():
            transfer(item, 0, place, place, sibling).wait_recv()

    def relay_far(item):
        arrive(item, 0)
        start(item, far_copies)

    def relay_near(item):
        arrive(item, 2)
        start(item, near_copies)

    def vis_copy(parts, step, landing_index):
        stage, listed, sent, received = parts
        target = lax.rem(me + step, n_source)
        return pltpu.make_async_remote_copy(
            src_ref=stage.at[lax.rem(target, n_shard)],
            dst_ref=listed.at[landing_index],
            send_sem=sent.at[step],
            recv_sem=received.at[step],
            device_id=peer(target),
            device_id_type=MESH,
        )

    def vis_start(parts):
        def one(step, carry):
            vis_copy(parts, step, me).start()
            return carry

        lax.fori_loop(1, n_source, one, 0)
        parts[1][me] = parts[0][my_shard]

    def vis_wait(parts):
        def one(step, carry):
            vis_copy(parts, step, lax.rem(me + n_source - step, n_source)).wait_recv()
            return carry

        lax.fori_loop(1, n_source, one, 0)

    def vis_finish(parts):
        def one(step, carry):
            vis_copy(parts, step, me).wait_send()
            return carry

        lax.fori_loop(1, n_source, one, 0)

    key_parts = (key_stage, key_listed, key_send, key_recv)
    query_parts = (query_stage, query_listed, query_send, query_recv)
    vis_start(key_parts)
    start(0, own_copies)
    vis_wait(key_parts)

    block_rows = n_shard * vis_block
    my_dest = my_seq.astype(jnp.float32)
    filled = jnp.zeros((aux_rows, 1), jnp.float32)
    for seq in range(n_seq):
        listed = key_listed[seq * n_shard:(seq + 1) * n_shard].reshape(block_rows, 3 * DH)
        dest = listed[:, 2 * DH:].astype(jnp.float32)
        dest_across = dest.T[0:1, :]
        earlier = jnp.where(dest[:, 0:1] == dest_across, same_ref[...], 0.0)
        rank = jnp.sum(earlier, axis=0, keepdims=True)
        placing = jnp.where(
            (slot_ref[...] == rank + float(seq * CAP)) & (dest_across == my_dest), pick_ref[...], 0.0
        )
        placing = placing.astype(jnp.bfloat16)
        placed[:, seq * block_rows:(seq + 1) * block_rows] = placing
        part = jnp.dot(placing, listed[:, :2 * DH], preferred_element_type=jnp.float32)
        slot_keys = part if seq == 0 else slot_keys + part
        filled = filled + jnp.sum(placing.astype(jnp.float32), axis=1, keepdims=True)
    aux_buf[REACH, 0:aux_rows] = slot_keys.astype(jnp.bfloat16)
    live_col[...] = jnp.broadcast_to(filled[:slot_count], live_col.shape)
    live_across = live_col[...].T[0:1, :]
    seg_row = seg_ref[...].reshape(1, rows).astype(jnp.float32) + 1.0
    text_tags = seg_row[:, :text]
    slot_tags = jnp.where(live_across > 0, seg_row[:, text:], 0.0)
    tag_rows = jnp.concatenate(
        [
            jnp.broadcast_to(text_tags, (8, text)),
            jnp.concatenate(
                [jnp.broadcast_to(slot_tags, (8, slot_count)), jnp.zeros((8, text - slot_count), jnp.float32)], axis=1
            ),
        ],
        axis=0,
    )
    aux_buf[REACH, aux_rows:] = tag_rows.astype(jnp.bfloat16)
    start(groups, own_copies)
    vis_start(query_parts)
    for item in range(1, groups):
        start(item, own_copies)

    relay_far(0)
    relay_far(groups)
    relay_near(0)
    relay_near(groups)
    if groups > 1:
        relay_far(1)
    arrive(groups, 1)
    arrive(groups, 3)

    total = key_all.shape[0]
    spare = pad - (REACH + 1) * slot_count
    all_tags = [aux_buf[place, aux_rows:].astype(jnp.float32)[0:1, :] for place in range(REACH)]
    all_tags.append(text_tags[:, :half])
    for place in range(REACH + 1):
        all_tags.append(aux_buf[place, aux_rows:].astype(jnp.float32)[8:9, :slot_count])
    if spare:
        all_tags.append(jnp.zeros((1, spare), jnp.float32))
    all_tags.append(text_tags[:, half:])
    tags = jnp.concatenate(all_tags, axis=1)
    name = lax.broadcasted_iota(jnp.int32, (DH, total), 0)
    at = lax.broadcasted_iota(jnp.int32, (DH, total), 1) - (slot_start + REACH * slot_count)
    differs = (name < OWN) & (name.astype(jnp.float32) + 1.0 != tags)
    own_slot = (name == OWN) & (at >= 0) & (at < slot_count)
    key_all[:, DH:] = jnp.where(differs | own_slot, FAR, 0.0).T.astype(jnp.bfloat16)
    together = text_mask.shape[2] // half
    slot_heads = max(1, min(GQ, together * half // slot_count))
    name = lax.broadcasted_iota(jnp.int32, (DH, rows), 0)
    at = lax.broadcasted_iota(jnp.int32, (DH, rows), 1)
    named = jnp.where((name.astype(jnp.float32) + 1.0 == seg_row) | ((name == OWN) & (at < text)), 1.0, 0.0)
    for part in range(2):
        narrow = named[:, part * half:(part + 1) * half].astype(jnp.bfloat16)
        text_mask[part] = jnp.concatenate([narrow] * together, axis=1)
    slot_mask[...] = jnp.concatenate([named[:, text:]] * slot_heads, axis=1).astype(jnp.bfloat16)
    ahead = lax.broadcasted_iota(jnp.int32, (half, half), 0) > lax.broadcasted_iota(jnp.int32, (half, half), 1)
    diagonal[...] = jnp.where(ahead, FAR, 0.0)
    val_all[DH:, :] = jnp.ones_like(val_all[DH:, :])
    scale = LOG2E * DH ** -0.5

    def turned(values):
        return values.astype(jnp.float32).T.astype(jnp.bfloat16)

    slot_end = slot_start + pad
    wide = jnp.concatenate([diagonal[...]] * together, axis=1)
    first_span = (0, slot_end, REACH * text, slot_start, wide)
    second_span = (half, total, slot_end, total, wide)

    def text_tile(group, heads, part, span):
        mine = slice(part * half, (part + 1) * half)

        def queries():
            rows_of = [text_ref[group, mine, k * DH:(k + 1) * DH] for k in heads]
            return jnp.concatenate([turned(jnp.concatenate(rows_of, axis=0)), text_mask[part]], axis=0)

        def store(result):
            result = result.astype(jnp.bfloat16)
            for number, k in enumerate(heads):
                out_ref[group, mine, k * DH:(k + 1) * DH] = result[number * half:(number + 1) * half]

        return queries, span, store

    def slot_tile(group, heads):
        extra = slot_order_ref[:, heads[0] * slot_count:(heads[-1] + 1) * slot_count]

        def queries():
            mine = pl.ds(pl.multiple_of(group * slot_count, slot_count), slot_count)
            rows_of = [slots[mine, k * DH:(k + 1) * DH] for k in heads]
            return jnp.concatenate([turned(jnp.concatenate(rows_of, axis=0)), slot_mask[...]], axis=0)

        def store(result):
            for number, k in enumerate(heads):
                kept = jnp.where(live_col[...] > 0, result[number * slot_count:(number + 1) * slot_count], 0.0)
                out_ref[group, text:, k * DH:(k + 1) * DH] = kept.astype(jnp.bfloat16)

        return queries, (text, total, slot_start, slot_end, extra), store

    vis_wait(query_parts)
    slots[...] = jnp.dot(
        placed[...], query_listed[...].reshape(n_source * vis_block, query_width), preferred_element_type=jnp.float32
    )
    score_slots, weight_slots = (score_even, score_odd), (weight_even, weight_odd)

    def one_group(group, carry):
        arrive(group, 1)
        arrive(group, 3)
        for place in range(REACH):
            key_all[place * text:(place + 1) * text, :DH] = kv_buf[group, place, :, :DH]
            val_all[:DH, place * text:(place + 1) * text] = turned(kv_buf[group, place, :, DH:])
        own = text_ref[group, :, query_width:]
        key_all[REACH * text:slot_start, :DH] = own[:half, :DH]
        val_all[:DH, REACH * text:slot_start] = turned(own[:half, DH:])
        key_all[slot_end:, :DH] = own[half:, :DH]
        val_all[:DH, slot_end:] = turned(own[half:, DH:])
        mine = pl.ds(pl.multiple_of(group * slot_count, slot_count), slot_count)
        slot_rows = [aux_buf[place, mine] for place in range(REACH + 1)]
        if spare:
            slot_rows.append(jnp.zeros((spare, 2 * DH), jnp.bfloat16))
        slot_rows = jnp.concatenate(slot_rows, axis=0)
        key_all[slot_start:slot_end, :DH] = slot_rows[:, :DH]
        val_all[:DH, slot_start:slot_end] = turned(slot_rows[:, DH:])

        tiles = []
        for head in range(0, GQ, slot_heads):
            tiles.append(slot_tile(group, range(head, head + slot_heads)))
        for head in range(0, GQ, together):
            heads = range(head, head + together)
            tiles.append(text_tile(group, heads, 0, first_span))
            tiles.append(text_tile(group, heads, 1, second_span))

        def score_steps(number):
            queries, (low, high, extra_low, extra_high, extra), _ = tiles[number]
            held = score_slots[number % 2]
            state = {"queries": queries(), "largest": None}

            def one(start_at, end_at):
                result = jnp.dot(key_all[start_at:end_at], state["queries"], preferred_element_type=jnp.float32)
                lanes = result.shape[1]
                for at in range(start_at, end_at, 128):
                    piece = result[at - start_at:at - start_at + 128]
                    if extra_low <= at < extra_high:
                        piece = piece + extra[at - extra_low:at - extra_low + 128]
                    held[at - low:at - low + 128, :lanes] = piece
                    part = jnp.max(piece.reshape(16, 8, lanes), axis=0)
                    state["largest"] = part if state["largest"] is None else jnp.maximum(state["largest"], part)

            middle = low + (high - low) // 256 * 128
            return [functools.partial(one, low, middle), functools.partial(one, middle, high)], state

        def weight_steps(number, state):
            low, high = tiles[number][1][:2]
            held, made = score_slots[number % 2], weight_slots[number % 2]
            lanes = state["largest"].shape[1]
            largest = jnp.max(state["largest"], axis=0, keepdims=True)

            def one(at, end):
                made[at:end, :lanes] = jnp.exp2((held[at:end, :lanes] - largest) * scale).astype(jnp.bfloat16)

            count = high - low
            return [functools.partial(one, at, min(at + 64, count)) for at in range(0, count, 64)], lanes

        def finish_tile(number, lanes):
            _, (low, high, *_), store = tiles[number]
            summed = jnp.dot(
                val_all[:, low:high], weight_slots[number % 2][:high - low, :lanes],
                preferred_element_type=jnp.float32,
            )
            store((summed[:DH] * (1.0 / summed[DH:DH + 1])).T)

        work, state = score_steps(0)
        for step in work:
            step()
        before = None
        for number in range(len(tiles)):
            if number == len(tiles) // 2:
                @pl.when(group + 1 < groups)
                def _():
                    relay_near(group + 1)

                @pl.when(group + 2 < groups)
                def _():
                    relay_far(group + 2)
            if before is not None:
                finish_tile(number - 1, before)
            weigh, lanes = weight_steps(number, state)
            score = []
            if number + 1 < len(tiles):
                score, state = score_steps(number + 1)
            done = 0
            for position, step in enumerate(score):
                step()
                until = (position + 1) * len(weigh) // len(score)
                for part in weigh[done:until]:
                    part()
                done = until
            for part in weigh[done:]:
                part()
            before = lanes
        finish_tile(len(tiles) - 1, before)
        return carry

    lax.fori_loop(0, groups, one_group, 0)

    for item in range(groups + 1):
        finish(item, own_copies + far_copies + near_copies)

    vis_finish(key_parts)
    vis_finish(query_parts)


def shards(mesh_shape, text_rows, vis_rows, vis_dest, segments):
    n_group, n_seq, n_shard = (mesh_shape[axis] for axis in ("group", "seq", "shard"))
    text, groups, width = text_rows.shape
    rows = segments.shape[0]
    slot_count = n_seq * CAP
    vis_count = vis_rows.shape[0]
    vis_block = up(vis_count * groups, 16)
    text_t = text_rows.transpose(1, 0, 2)
    index = np.arange(n_shard * vis_block)
    within = index % vis_block
    valid = within < vis_count * groups
    head = within % groups
    same = (head[:, None] == head[None, :]) & (index[:, None] < index[None, :]) & valid[:, None] & valid[None, :]
    place = np.arange(groups * slot_count)
    pick = (place[:, None] // slot_count == head[None, :]) & valid[None, :]
    slot = np.broadcast_to((place % slot_count)[:, None], pick.shape)

    pad = up((REACH + 1) * slot_count, 128)
    own = np.arange(pad) - REACH * slot_count
    behind = (own[:, None] > np.arange(GQ * slot_count)[None, :] % slot_count) & (own < slot_count)[:, None]
    keys = (REACH + 1) * text + pad
    aux_rows = groups * slot_count + 16
    n_source = n_seq * n_shard
    lanes = TOGETHER * (text // 2)
    vmem = pl.BlockSpec(memory_space=pltpu.VMEM)
    result = pl.pallas_call(
        functools.partial(kernel, n_group, n_seq, n_shard),
        out_shape=jax.ShapeDtypeStruct((groups, rows, GQ * DH), jnp.bfloat16),
        in_specs=[vmem] * 8,
        out_specs=vmem,
        scratch_shapes=[
            pltpu.VMEM((groups, REACH, text, 2 * DH), jnp.bfloat16),
            pltpu.VMEM((REACH + 1, aux_rows, 2 * DH), jnp.bfloat16),
            pltpu.VMEM((n_shard, vis_block, 3 * DH), jnp.bfloat16),
            pltpu.VMEM((n_source, vis_block, 3 * DH), jnp.bfloat16),
            pltpu.VMEM((n_shard, vis_block, GQ * DH), jnp.bfloat16),
            pltpu.VMEM((n_source, vis_block, GQ * DH), jnp.bfloat16),
            pltpu.VMEM((groups * slot_count, n_source * vis_block), jnp.bfloat16),
            pltpu.VMEM((keys, 2 * DH), jnp.bfloat16),
            pltpu.VMEM((DH + 16, keys), jnp.bfloat16),
            pltpu.VMEM((2, DH, lanes), jnp.bfloat16),
            pltpu.VMEM((DH, min(GQ * slot_count, lanes)), jnp.bfloat16),
            pltpu.VMEM((text // 2, text // 2), jnp.float32),
            pltpu.VMEM((groups * slot_count, GQ * DH), jnp.float32),
            pltpu.VMEM((slot_count, DH), jnp.float32),
            pltpu.VMEM((keys - text // 2, lanes), jnp.float32),
            pltpu.VMEM((keys - text // 2, lanes), jnp.float32),
            pltpu.VMEM((keys - text // 2, lanes), jnp.bfloat16),
            pltpu.VMEM((keys - text // 2, lanes), jnp.bfloat16),
            pltpu.SemaphoreType.DMA((groups + 1, 6)),
            pltpu.SemaphoreType.DMA((groups + 1, REACH)),
            pltpu.SemaphoreType.DMA((n_source,)),
            pltpu.SemaphoreType.DMA((n_source,)),
            pltpu.SemaphoreType.DMA((n_source,)),
            pltpu.SemaphoreType.DMA((n_source,)),
        ],
        compiler_params=pltpu.CompilerParams(
            collective_id=0, has_side_effects=True, vmem_limit_bytes=36 * 1024 * 1024
        ),
    )(
        text_t,
        vis_rows,
        jnp.broadcast_to(vis_dest, (vis_count, DH)),
        segments,
        jnp.asarray(same, jnp.float32),
        jnp.asarray(pick, jnp.float32),
        jnp.asarray(slot, jnp.float32),
        jnp.asarray(np.where(behind, FAR, 0.0), jnp.float32),
    )
    return result.transpose(1, 0, 2)


def solution(mesh):
    placed = (
        P(("group", "seq"), "shard", None),
        P(("group", "seq", "shard"), None, None),
        P(("group", "seq", "shard"), None),
        P(("group", "seq")),
    )
    return jax.shard_map(
        functools.partial(shards, dict(mesh.shape)),
        mesh=mesh,
        in_specs=placed,
        out_specs=P(("group", "seq"), "shard", None),
        check_vma=False,
    )
```

```python
import functools
import math

import jax
import jax.numpy as jnp
import numpy as np
from jax import lax
from jax.experimental import pallas as pl
from jax.experimental.pallas import tpu as pltpu
from jax.sharding import PartitionSpec as P

GQ = 8
DH = 128
CAP = 4
REACH = 4
FAR = -(2.0 ** 100)
OWN = 120
TOGETHER = 2
LOG2E = math.log2(math.e)
MESH = pl.DeviceIdType.MESH


def up(value, step):
    return -(-value // step) * step


def kernel(
    n_group, n_seq, n_shard, text_ref, vis_ref, dest_ref, seg_ref, same_ref, pick_ref, slot_ref,
    slot_order_ref, out_ref, kv_buf, aux_buf, key_stage, key_listed, query_stage, query_listed, placed, key_all, val_all,
    text_mask, slot_mask, diagonal, slots, live_col,
    score_even, score_odd, weight_even, weight_odd,
    send_sem, recv_sem, key_send, key_recv, query_send, query_recv,
):
    groups, text, width = text_ref.shape
    query_width = GQ * DH
    rows = out_ref.shape[1]
    slot_count = rows - text
    half = text // 2
    pad = key_all.shape[0] - (REACH + 1) * text
    slot_start = REACH * text + half
    vis_count, vis_block = vis_ref.shape[0], key_stage.shape[1]
    n_source = n_seq * n_shard
    blocks = n_group * n_seq
    aux_rows = groups * slot_count

    my_group, my_seq, my_shard = lax.axis_index("group"), lax.axis_index("seq"), lax.axis_index("shard")
    here = my_group * n_seq + my_seq
    odd = lax.rem(here, 2)
    upper = lax.rem(here // 2, 2)
    sibling = here + 1 - 2 * odd
    partner = here + 2 - 4 * upper
    me = my_seq * n_shard + my_shard

    def device(block):
        return (block // n_seq, lax.rem(block, n_seq), my_shard)

    def peer(index):
        return (my_group, index // n_shard, lax.rem(index, n_shard))

    barrier = pltpu.get_barrier_semaphore()

    vis_wide = vis_ref[...].astype(jnp.float32)
    dest_wide = dest_ref[...].reshape(1, vis_count).astype(jnp.float32)
    for shard in range(n_shard):
        listed = [vis_wide[row, shard * groups:(shard + 1) * groups] for row in range(vis_count)]
        names = [jnp.broadcast_to(dest_wide[:, row:row + 1], (groups, DH)) for row in range(vis_count)]
        if vis_block > vis_count * groups:
            listed.append(jnp.zeros((vis_block - vis_count * groups, width), jnp.float32))
            names.append(jnp.zeros((vis_block - vis_count * groups, DH), jnp.float32))
        listed = jnp.concatenate(listed, axis=0).astype(jnp.bfloat16)
        query_stage[shard] = listed[:, :query_width]
        key_stage[shard, :, :2 * DH] = listed[:, query_width:]
        key_stage[shard, :, 2 * DH:] = jnp.concatenate(names, axis=0).astype(jnp.bfloat16)

    def greet(step, carry):
        pl.semaphore_signal(barrier, inc=1, device_id=peer(lax.rem(me + step, n_source)), device_id_type=MESH)
        return carry

    lax.fori_loop(1, n_source, greet, 0)
    pl.semaphore_signal(barrier, inc=1, device_id=device(sibling), device_id_type=MESH)
    pl.semaphore_signal(barrier, inc=1, device_id=device(partner), device_id_type=MESH)

    @pl.when(here >= REACH)
    def _():
        pl.semaphore_signal(barrier, inc=1, device_id=device(here - REACH), device_id_type=MESH)

    for place in range(REACH):
        @pl.when(here < REACH - place)
        def _():
            kv_buf[:, place] = jnp.zeros_like(kv_buf[:, place])
            aux_buf[place] = jnp.zeros_like(aux_buf[place])

    pl.semaphore_wait(barrier, n_source + 1 + (here + REACH < blocks).astype(jnp.int32))

    def is_aux(item):
        return isinstance(item, int) and item == groups

    def landing(item, place):
        return aux_buf.at[place] if is_aux(item) else kv_buf.at[item, place]

    def source(item, place):
        if place < REACH:
            return landing(item, place)
        if is_aux(item):
            return aux_buf.at[REACH]
        return text_ref.at[item, :, pl.ds(query_width, 2 * DH)]

    def transfer(item, number, place, target_place, target):
        return pltpu.make_async_remote_copy(
            src_ref=source(item, place),
            dst_ref=landing(item, target_place),
            send_sem=send_sem.at[item, number],
            recv_sem=recv_sem.at[item, target_place],
            device_id=device(target),
            device_id_type=MESH,
        )

    own_copies = [
        (here + REACH < blocks, 0, 4, 0, here + REACH),
        (upper == 0, 1, 4, 2, here + 2),
        (odd == 0, 2, 4, 3, here + 1),
    ]
    far_copies = [
        ((here >= 4) & (upper == 1), 3, 0, 2, here - 2),
        ((here >= 4) & (odd == 1), 4, 0, 1, here - 1),
    ]
    near_copies = [
        ((here >= 2) & (odd == 0), 5, 2, 1, here + 1),
        ((here >= 2) & (odd == 1), 5, 2, 3, here - 1),
    ]

    def start(item, copies):
        for condition, number, place, target_place, target in copies:
            @pl.when(condition)
            def _():
                transfer(item, number, place, target_place, target).start()

    def finish(item, copies):
        for condition, number, place, target_place, target in copies:
            @pl.when(condition)
            def _():
                transfer(item, number, place, target_place, target).wait_send()

    def arrive(item, place):
        @pl.when(here >= REACH - place)
        def _():
            transfer(item, 0, place, place, sibling).wait_recv()

    def relay_far(item):
        arrive(item, 0)
        start(item, far_copies)

    def relay_near(item):
        arrive(item, 2)
        start(item, near_copies)

    def vis_copy(parts, step, landing_index):
        stage, listed, sent, received = parts
        target = lax.rem(me + step, n_source)
        return pltpu.make_async_remote_copy(
            src_ref=stage.at[lax.rem(target, n_shard)],
            dst_ref=listed.at[landing_index],
            send_sem=sent.at[step],
            recv_sem=received.at[step],
            device_id=peer(target),
            device_id_type=MESH,
        )

    def vis_start(parts):
        def one(step, carry):
            vis_copy(parts, step, me).start()
            return carry

        lax.fori_loop(1, n_source, one, 0)
        parts[1][me] = parts[0][my_shard]

    def vis_wait(parts):
        def one(step, carry):
            vis_copy(parts, step, lax.rem(me + n_source - step, n_source)).wait_recv()
            return carry

        lax.fori_loop(1, n_source, one, 0)

    def vis_finish(parts):
        def one(step, carry):
            vis_copy(parts, step, me).wait_send()
            return carry

        lax.fori_loop(1, n_source, one, 0)

    key_parts = (key_stage, key_listed, key_send, key_recv)
    query_parts = (query_stage, query_listed, query_send, query_recv)
    vis_start(key_parts)
    start(0, own_copies)

    seg_row = seg_ref[...].reshape(1, rows).astype(jnp.float32) + 1.0
    together = text_mask.shape[2] // half
    slot_heads = max(1, min(GQ, together * half // slot_count))
    name = lax.broadcasted_iota(jnp.int32, (DH, rows), 0)
    at = lax.broadcasted_iota(jnp.int32, (DH, rows), 1)
    named = jnp.where((name.astype(jnp.float32) + 1.0 == seg_row) | ((name == OWN) & (at < text)), 1.0, 0.0)
    for part in range(2):
        narrow = named[:, part * half:(part + 1) * half].astype(jnp.bfloat16)
        text_mask[part] = jnp.concatenate([narrow] * together, axis=1)
    slot_mask[...] = jnp.concatenate([named[:, text:]] * slot_heads, axis=1).astype(jnp.bfloat16)
    ahead = lax.broadcasted_iota(jnp.int32, (half, half), 0) > lax.broadcasted_iota(jnp.int32, (half, half), 1)
    diagonal[...] = jnp.where(ahead, FAR, 0.0)
    val_all[DH:, :] = jnp.ones_like(val_all[DH:, :])

    vis_wait(key_parts)

    block_rows = n_shard * vis_block
    my_dest = my_seq.astype(jnp.float32)
    filled = jnp.zeros((aux_rows, 1), jnp.float32)
    for seq in range(n_seq):
        listed = key_listed[seq * n_shard:(seq + 1) * n_shard].reshape(block_rows, 3 * DH)
        dest = listed[:, 2 * DH:].astype(jnp.float32)
        dest_across = dest.T[0:1, :]
        earlier = jnp.where(dest[:, 0:1] == dest_across, same_ref[...], 0.0)
        rank = jnp.sum(earlier, axis=0, keepdims=True)
        placing = jnp.where(
            (slot_ref[...] == rank + float(seq * CAP)) & (dest_across == my_dest), pick_ref[...], 0.0
        )
        placing = placing.astype(jnp.bfloat16)
        placed[:, seq * block_rows:(seq + 1) * block_rows] = placing
        part = jnp.dot(placing, listed[:, :2 * DH], preferred_element_type=jnp.float32)
        slot_keys = part if seq == 0 else slot_keys + part
        filled = filled + jnp.sum(placing.astype(jnp.float32), axis=1, keepdims=True)
    aux_buf[REACH, 0:aux_rows] = slot_keys.astype(jnp.bfloat16)
    live_col[...] = jnp.broadcast_to(filled[:slot_count], live_col.shape)
    live_across = live_col[...].T[0:1, :]
    text_tags = seg_row[:, :text]
    slot_tags = jnp.where(live_across > 0, seg_row[:, text:], 0.0)
    tag_rows = jnp.concatenate(
        [
            jnp.broadcast_to(text_tags, (8, text)),
            jnp.concatenate(
                [jnp.broadcast_to(slot_tags, (8, slot_count)), jnp.zeros((8, text - slot_count), jnp.float32)], axis=1
            ),
        ],
        axis=0,
    )
    aux_buf[REACH, aux_rows:] = tag_rows.astype(jnp.bfloat16)
    start(groups, own_copies)

    relay_far(0)
    relay_far(groups)
    vis_start(query_parts)
    if groups > 1:
        start(1, own_copies)
    relay_near(0)
    relay_near(groups)
    for item in range(2, groups):
        start(item, own_copies)
    arrive(groups, 1)
    arrive(groups, 3)

    total = key_all.shape[0]
    spare = pad - (REACH + 1) * slot_count
    all_tags = [aux_buf[place, aux_rows:].astype(jnp.float32)[0:1, :] for place in range(REACH)]
    all_tags.append(text_tags[:, :half])
    for place in range(REACH + 1):
        all_tags.append(aux_buf[place, aux_rows:].astype(jnp.float32)[8:9, :slot_count])
    if spare:
        all_tags.append(jnp.zeros((1, spare), jnp.float32))
    all_tags.append(text_tags[:, half:])
    tags = jnp.concatenate(all_tags, axis=1)
    name = lax.broadcasted_iota(jnp.int32, (DH, total), 0)
    at = lax.broadcasted_iota(jnp.int32, (DH, total), 1) - (slot_start + REACH * slot_count)
    differs = (name < OWN) & (name.astype(jnp.float32) + 1.0 != tags)
    own_slot = (name == OWN) & (at >= 0) & (at < slot_count)
    key_all[:, DH:] = jnp.where(differs | own_slot, FAR, 0.0).T.astype(jnp.bfloat16)
    scale = LOG2E * DH ** -0.5

    def turned(values):
        return values.astype(jnp.float32).T.astype(jnp.bfloat16)

    slot_end = slot_start + pad
    wide = jnp.concatenate([diagonal[...]] * together, axis=1)
    first_span = (0, slot_end, REACH * text, slot_start, wide)
    second_span = (half, total, slot_end, total, wide)

    def text_tile(group, heads, part, span):
        mine = slice(part * half, (part + 1) * half)

        def queries():
            rows_of = [text_ref[group, mine, k * DH:(k + 1) * DH] for k in heads]
            return jnp.concatenate([turned(jnp.concatenate(rows_of, axis=0)), text_mask[part]], axis=0)

        def store(result):
            result = result.astype(jnp.bfloat16)
            for number, k in enumerate(heads):
                out_ref[group, mine, k * DH:(k + 1) * DH] = result[number * half:(number + 1) * half]

        return queries, span, store

    def slot_tile(group, heads):
        extra = slot_order_ref[:, heads[0] * slot_count:(heads[-1] + 1) * slot_count]

        def queries():
            mine = pl.ds(pl.multiple_of(group * slot_count, slot_count), slot_count)
            rows_of = [slots[mine, k * DH:(k + 1) * DH] for k in heads]
            return jnp.concatenate([turned(jnp.concatenate(rows_of, axis=0)), slot_mask[...]], axis=0)

        def store(result):
            for number, k in enumerate(heads):
                kept = jnp.where(live_col[...] > 0, result[number * slot_count:(number + 1) * slot_count], 0.0)
                out_ref[group, text:, k * DH:(k + 1) * DH] = kept.astype(jnp.bfloat16)

        return queries, (text, total, slot_start, slot_end, extra), store

    vis_wait(query_parts)
    slots[...] = jnp.dot(
        placed[...], query_listed[...].reshape(n_source * vis_block, query_width), preferred_element_type=jnp.float32
    )
    score_slots, weight_slots = (score_even, score_odd), (weight_even, weight_odd)

    def one_group(group, carry):
        arrive(group, 1)
        arrive(group, 3)
        for place in range(REACH):
            key_all[place * text:(place + 1) * text, :DH] = kv_buf[group, place, :, :DH]
            val_all[:DH, place * text:(place + 1) * text] = turned(kv_buf[group, place, :, DH:])
        own = text_ref[group, :, query_width:]
        key_all[REACH * text:slot_start, :DH] = own[:half, :DH]
        val_all[:DH, REACH * text:slot_start] = turned(own[:half, DH:])
        key_all[slot_end:, :DH] = own[half:, :DH]
        val_all[:DH, slot_end:] = turned(own[half:, DH:])
        mine = pl.ds(pl.multiple_of(group * slot_count, slot_count), slot_count)
        slot_rows = [aux_buf[place, mine] for place in range(REACH + 1)]
        if spare:
            slot_rows.append(jnp.zeros((spare, 2 * DH), jnp.bfloat16))
        slot_rows = jnp.concatenate(slot_rows, axis=0)
        key_all[slot_start:slot_end, :DH] = slot_rows[:, :DH]
        val_all[:DH, slot_start:slot_end] = turned(slot_rows[:, DH:])

        tiles = []
        for head in range(0, GQ, slot_heads):
            tiles.append(slot_tile(group, range(head, head + slot_heads)))
        for head in range(0, GQ, together):
            heads = range(head, head + together)
            tiles.append(text_tile(group, heads, 0, first_span))
            tiles.append(text_tile(group, heads, 1, second_span))

        def score_steps(number):
            queries, (low, high, extra_low, extra_high, extra), _ = tiles[number]
            held = score_slots[number % 2]
            state = {"queries": queries(), "largest": None}

            def one(start_at, end_at):
                result = jnp.dot(key_all[start_at:end_at], state["queries"], preferred_element_type=jnp.float32)
                lanes = result.shape[1]
                for at in range(start_at, end_at, 128):
                    piece = result[at - start_at:at - start_at + 128]
                    if extra_low <= at < extra_high:
                        piece = piece + extra[at - extra_low:at - extra_low + 128]
                    held[at - low:at - low + 128, :lanes] = piece
                    part = jnp.max(piece.reshape(16, 8, lanes), axis=0)
                    state["largest"] = part if state["largest"] is None else jnp.maximum(state["largest"], part)

            middle = low + (high - low) // 256 * 128
            return [functools.partial(one, low, middle), functools.partial(one, middle, high)], state

        def weight_steps(number, state):
            low, high = tiles[number][1][:2]
            held, made = score_slots[number % 2], weight_slots[number % 2]
            lanes = state["largest"].shape[1]
            largest = jnp.max(state["largest"], axis=0, keepdims=True) * scale

            def one(at, end):
                made[at:end, :lanes] = jnp.exp2(held[at:end, :lanes] * scale - largest).astype(jnp.bfloat16)

            count = high - low
            return [functools.partial(one, at, min(at + 64, count)) for at in range(0, count, 64)], lanes

        def finish_tile(number, lanes):
            _, (low, high, *_), store = tiles[number]
            summed = jnp.dot(
                val_all[:, low:high], weight_slots[number % 2][:high - low, :lanes],
                preferred_element_type=jnp.float32,
            )
            store((summed[:DH] * (1.0 / summed[DH:DH + 1])).T)

        work, state = score_steps(0)
        for step in work:
            step()
        before = None
        for number in range(len(tiles)):
            if number == len(tiles) * 4 // 9:
                @pl.when(group + 1 < groups)
                def _():
                    relay_far(group + 1)
            if number == len(tiles) * 7 // 9:
                @pl.when(group + 1 < groups)
                def _():
                    relay_near(group + 1)
            if before is not None:
                finish_tile(number - 1, before)
            weigh, lanes = weight_steps(number, state)
            score = []
            if number + 1 < len(tiles):
                score, state = score_steps(number + 1)
            done = 0
            for position, step in enumerate(score):
                step()
                until = (position + 1) * len(weigh) // len(score)
                for part in weigh[done:until]:
                    part()
                done = until
            for part in weigh[done:]:
                part()
            before = lanes
        finish_tile(len(tiles) - 1, before)
        return carry

    lax.fori_loop(0, groups, one_group, 0)

    for item in range(groups + 1):
        finish(item, own_copies + far_copies + near_copies)

    vis_finish(key_parts)
    vis_finish(query_parts)


def shards(mesh_shape, text_rows, vis_rows, vis_dest, segments):
    n_group, n_seq, n_shard = (mesh_shape[axis] for axis in ("group", "seq", "shard"))
    text, groups, width = text_rows.shape
    rows = segments.shape[0]
    slot_count = n_seq * CAP
    vis_count = vis_rows.shape[0]
    vis_block = up(vis_count * groups, 16)
    text_t = text_rows.transpose(1, 0, 2)
    index = np.arange(n_shard * vis_block)
    within = index % vis_block
    valid = within < vis_count * groups
    head = within % groups
    same = (head[:, None] == head[None, :]) & (index[:, None] < index[None, :]) & valid[:, None] & valid[None, :]
    place = np.arange(groups * slot_count)
    pick = (place[:, None] // slot_count == head[None, :]) & valid[None, :]
    slot = np.broadcast_to((place % slot_count)[:, None], pick.shape)

    pad = up((REACH + 1) * slot_count, 128)
    own = np.arange(pad) - REACH * slot_count
    behind = (own[:, None] > np.arange(GQ * slot_count)[None, :] % slot_count) & (own < slot_count)[:, None]
    keys = (REACH + 1) * text + pad
    aux_rows = groups * slot_count + 16
    n_source = n_seq * n_shard
    lanes = TOGETHER * (text // 2)
    vmem = pl.BlockSpec(memory_space=pltpu.VMEM)
    result = pl.pallas_call(
        functools.partial(kernel, n_group, n_seq, n_shard),
        out_shape=jax.ShapeDtypeStruct((groups, rows, GQ * DH), jnp.bfloat16),
        in_specs=[vmem] * 8,
        out_specs=vmem,
        scratch_shapes=[
            pltpu.VMEM((groups, REACH, text, 2 * DH), jnp.bfloat16),
            pltpu.VMEM((REACH + 1, aux_rows, 2 * DH), jnp.bfloat16),
            pltpu.VMEM((n_shard, vis_block, 3 * DH), jnp.bfloat16),
            pltpu.VMEM((n_source, vis_block, 3 * DH), jnp.bfloat16),
            pltpu.VMEM((n_shard, vis_block, GQ * DH), jnp.bfloat16),
            pltpu.VMEM((n_source, vis_block, GQ * DH), jnp.bfloat16),
            pltpu.VMEM((groups * slot_count, n_source * vis_block), jnp.bfloat16),
            pltpu.VMEM((keys, 2 * DH), jnp.bfloat16),
            pltpu.VMEM((DH + 16, keys), jnp.bfloat16),
            pltpu.VMEM((2, DH, lanes), jnp.bfloat16),
            pltpu.VMEM((DH, min(GQ * slot_count, lanes)), jnp.bfloat16),
            pltpu.VMEM((text // 2, text // 2), jnp.float32),
            pltpu.VMEM((groups * slot_count, GQ * DH), jnp.float32),
            pltpu.VMEM((slot_count, DH), jnp.float32),
            pltpu.VMEM((keys - text // 2, lanes), jnp.float32),
            pltpu.VMEM((keys - text // 2, lanes), jnp.float32),
            pltpu.VMEM((keys - text // 2, lanes), jnp.bfloat16),
            pltpu.VMEM((keys - text // 2, lanes), jnp.bfloat16),
            pltpu.SemaphoreType.DMA((groups + 1, 6)),
            pltpu.SemaphoreType.DMA((groups + 1, REACH)),
            pltpu.SemaphoreType.DMA((n_source,)),
            pltpu.SemaphoreType.DMA((n_source,)),
            pltpu.SemaphoreType.DMA((n_source,)),
            pltpu.SemaphoreType.DMA((n_source,)),
        ],
        compiler_params=pltpu.CompilerParams(
            collective_id=0, has_side_effects=True, vmem_limit_bytes=36 * 1024 * 1024
        ),
    )(
        text_t,
        vis_rows,
        vis_dest.reshape(vis_count),
        segments,
        jnp.asarray(same, jnp.float32),
        jnp.asarray(pick, jnp.float32),
        jnp.asarray(slot, jnp.float32),
        jnp.asarray(np.where(behind, FAR, 0.0), jnp.float32),
    )
    return result.transpose(1, 0, 2)


def solution(mesh):
    placed = (
        P(("group", "seq"), "shard", None),
        P(("group", "seq", "shard"), None, None),
        P(("group", "seq", "shard"), None),
        P(("group", "seq")),
    )
    return jax.shard_map(
        functools.partial(shards, dict(mesh.shape)),
        mesh=mesh,
        in_specs=placed,
        out_specs=P(("group", "seq"), "shard", None),
        check_vma=False,
    )
```

```python
import functools
import math

import jax
import jax.numpy as jnp
import numpy as np
from jax import lax
from jax.experimental import pallas as pl
from jax.experimental.pallas import tpu as pltpu
from jax.sharding import PartitionSpec as P

GQ = 8
DH = 128
CAP = 4
REACH = 4
FAR = -(2.0 ** 100)
OWN = 120
TOGETHER = 2
LOG2E = math.log2(math.e)
MESH = pl.DeviceIdType.MESH


def up(value, step):
    return -(-value // step) * step


def kernel(
    n_group, n_seq, n_shard, text_ref, vis_ref, dest_ref, seg_ref, same_ref, pick_ref, slot_ref,
    slot_order_ref, out_ref, kv_buf, aux_buf, key_stage, key_listed, query_stage, query_listed, placed, key_all, val_all,
    text_mask, slot_mask, diagonal, slots, live_col,
    score_even, score_odd, weight_even, weight_odd,
    send_sem, recv_sem, key_send, key_recv, query_send, query_recv,
):
    groups, text, width = text_ref.shape
    query_width = GQ * DH
    rows = out_ref.shape[1]
    slot_count = rows - text
    half = text // 2
    pad = key_all.shape[0] - (REACH + 1) * text
    slot_start = REACH * text + half
    vis_count, vis_block = vis_ref.shape[0], key_stage.shape[1]
    n_source = n_seq * n_shard
    blocks = n_group * n_seq
    aux_rows = groups * slot_count

    my_group, my_seq, my_shard = lax.axis_index("group"), lax.axis_index("seq"), lax.axis_index("shard")
    here = my_group * n_seq + my_seq
    odd = lax.rem(here, 2)
    upper = lax.rem(here // 2, 2)
    sibling = here + 1 - 2 * odd
    partner = here + 2 - 4 * upper
    me = my_seq * n_shard + my_shard

    def device(block):
        return (block // n_seq, lax.rem(block, n_seq), my_shard)

    def peer(index):
        return (my_group, index // n_shard, lax.rem(index, n_shard))

    barrier = pltpu.get_barrier_semaphore()

    vis_wide = vis_ref[...].astype(jnp.float32)
    dest_wide = dest_ref[...].reshape(1, vis_count).astype(jnp.float32)
    for shard in range(n_shard):
        listed = [vis_wide[row, shard * groups:(shard + 1) * groups] for row in range(vis_count)]
        names = [jnp.broadcast_to(dest_wide[:, row:row + 1], (groups, DH)) for row in range(vis_count)]
        if vis_block > vis_count * groups:
            listed.append(jnp.zeros((vis_block - vis_count * groups, width), jnp.float32))
            names.append(jnp.zeros((vis_block - vis_count * groups, DH), jnp.float32))
        listed = jnp.concatenate(listed, axis=0).astype(jnp.bfloat16)
        query_stage[shard] = listed[:, :query_width]
        key_stage[shard, :, :2 * DH] = listed[:, query_width:]
        key_stage[shard, :, 2 * DH:] = jnp.concatenate(names, axis=0).astype(jnp.bfloat16)

    def greet(step, carry):
        pl.semaphore_signal(barrier, inc=1, device_id=peer(lax.rem(me + step, n_source)), device_id_type=MESH)
        return carry

    lax.fori_loop(1, n_source, greet, 0)
    pl.semaphore_signal(barrier, inc=1, device_id=device(sibling), device_id_type=MESH)
    pl.semaphore_signal(barrier, inc=1, device_id=device(partner), device_id_type=MESH)

    @pl.when(here >= REACH)
    def _():
        pl.semaphore_signal(barrier, inc=1, device_id=device(here - REACH), device_id_type=MESH)

    for place in range(REACH):
        @pl.when(here < REACH - place)
        def _():
            kv_buf[:, place] = jnp.zeros_like(kv_buf[:, place])
            aux_buf[place] = jnp.zeros_like(aux_buf[place])

    pl.semaphore_wait(barrier, n_source + 1 + (here + REACH < blocks).astype(jnp.int32))

    def is_aux(item):
        return isinstance(item, int) and item == groups

    def landing(item, place):
        return aux_buf.at[place] if is_aux(item) else kv_buf.at[item, place]

    def source(item, place):
        if place < REACH:
            return landing(item, place)
        if is_aux(item):
            return aux_buf.at[REACH]
        return text_ref.at[item, :, pl.ds(query_width, 2 * DH)]

    def transfer(item, number, place, target_place, target):
        return pltpu.make_async_remote_copy(
            src_ref=source(item, place),
            dst_ref=landing(item, target_place),
            send_sem=send_sem.at[item, number],
            recv_sem=recv_sem.at[item, target_place],
            device_id=device(target),
            device_id_type=MESH,
        )

    own_copies = [
        (here + REACH < blocks, 0, 4, 0, here + REACH),
        (upper == 0, 1, 4, 2, here + 2),
        (odd == 0, 2, 4, 3, here + 1),
    ]
    far_copies = [
        ((here >= 4) & (upper == 1), 3, 0, 2, here - 2),
        ((here >= 4) & (odd == 1), 4, 0, 1, here - 1),
    ]
    near_copies = [
        ((here >= 2) & (odd == 0), 5, 2, 1, here + 1),
        ((here >= 2) & (odd == 1), 5, 2, 3, here - 1),
    ]

    def start(item, copies):
        for condition, number, place, target_place, target in copies:
            @pl.when(condition)
            def _():
                transfer(item, number, place, target_place, target).start()

    def finish(item, copies):
        for condition, number, place, target_place, target in copies:
            @pl.when(condition)
            def _():
                transfer(item, number, place, target_place, target).wait_send()

    def arrive(item, place):
        @pl.when(here >= REACH - place)
        def _():
            transfer(item, 0, place, place, sibling).wait_recv()

    def relay_far(item):
        arrive(item, 0)
        start(item, far_copies)

    def relay_near(item):
        arrive(item, 2)
        start(item, near_copies)

    def vis_copy(parts, step, landing_index):
        stage, listed, sent, received = parts
        target = lax.rem(me + step, n_source)
        return pltpu.make_async_remote_copy(
            src_ref=stage.at[lax.rem(target, n_shard)],
            dst_ref=listed.at[landing_index],
            send_sem=sent.at[step],
            recv_sem=received.at[step],
            device_id=peer(target),
            device_id_type=MESH,
        )

    def vis_start(parts):
        def one(step, carry):
            vis_copy(parts, step, me).start()
            return carry

        lax.fori_loop(1, n_source, one, 0)
        parts[1][me] = parts[0][my_shard]

    def vis_wait(parts):
        def one(step, carry):
            vis_copy(parts, step, lax.rem(me + n_source - step, n_source)).wait_recv()
            return carry

        lax.fori_loop(1, n_source, one, 0)

    def vis_finish(parts):
        def one(step, carry):
            vis_copy(parts, step, me).wait_send()
            return carry

        lax.fori_loop(1, n_source, one, 0)

    key_parts = (key_stage, key_listed, key_send, key_recv)
    query_parts = (query_stage, query_listed, query_send, query_recv)
    vis_start(key_parts)
    start(0, own_copies)

    seg_row = seg_ref[...].reshape(1, rows).astype(jnp.float32) + 1.0
    together = text_mask.shape[2] // half
    slot_heads = max(1, min(GQ, together * half // slot_count))
    name = lax.broadcasted_iota(jnp.int32, (DH, rows), 0)
    at = lax.broadcasted_iota(jnp.int32, (DH, rows), 1)
    named = jnp.where((name.astype(jnp.float32) + 1.0 == seg_row) | ((name == OWN) & (at < text)), 1.0, 0.0)
    for part in range(2):
        narrow = named[:, part * half:(part + 1) * half].astype(jnp.bfloat16)
        text_mask[part] = jnp.concatenate([narrow] * together, axis=1)
    slot_mask[...] = jnp.concatenate([named[:, text:]] * slot_heads, axis=1).astype(jnp.bfloat16)
    ahead = lax.broadcasted_iota(jnp.int32, (half, half), 0) > lax.broadcasted_iota(jnp.int32, (half, half), 1)
    diagonal[...] = jnp.where(ahead, FAR, 0.0)
    val_all[DH:, :] = jnp.ones_like(val_all[DH:, :])

    vis_wait(key_parts)

    block_rows = n_shard * vis_block
    my_dest = my_seq.astype(jnp.float32)
    filled = jnp.zeros((aux_rows, 1), jnp.float32)
    for seq in range(n_seq):
        listed = key_listed[seq * n_shard:(seq + 1) * n_shard].reshape(block_rows, 3 * DH)
        dest = listed[:, 2 * DH:].astype(jnp.float32)
        dest_across = dest.T[0:1, :]
        earlier = jnp.where(dest[:, 0:1] == dest_across, same_ref[...], 0.0)
        rank = jnp.sum(earlier, axis=0, keepdims=True)
        placing = jnp.where(
            (slot_ref[...] == rank + float(seq * CAP)) & (dest_across == my_dest), pick_ref[...], 0.0
        )
        placing = placing.astype(jnp.bfloat16)
        placed[:, seq * block_rows:(seq + 1) * block_rows] = placing
        part = jnp.dot(placing, listed[:, :2 * DH], preferred_element_type=jnp.float32)
        slot_keys = part if seq == 0 else slot_keys + part
        filled = filled + jnp.sum(placing.astype(jnp.float32), axis=1, keepdims=True)
    aux_buf[REACH, 0:aux_rows] = slot_keys.astype(jnp.bfloat16)
    live_col[...] = jnp.broadcast_to(filled[:slot_count], live_col.shape)
    live_across = live_col[...].T[0:1, :]
    text_tags = seg_row[:, :text]
    slot_tags = jnp.where(live_across > 0, seg_row[:, text:], 0.0)
    tag_rows = jnp.concatenate(
        [
            jnp.broadcast_to(text_tags, (8, text)),
            jnp.concatenate(
                [jnp.broadcast_to(slot_tags, (8, slot_count)), jnp.zeros((8, text - slot_count), jnp.float32)], axis=1
            ),
        ],
        axis=0,
    )
    aux_buf[REACH, aux_rows:] = tag_rows.astype(jnp.bfloat16)
    start(groups, own_copies)
    vis_start(query_parts)
    for item in range(1, groups):
        start(item, own_copies)

    relay_far(0)
    relay_far(groups)
    relay_near(0)
    relay_near(groups)
    if groups > 1:
        relay_far(1)
    arrive(groups, 1)
    arrive(groups, 3)

    total = key_all.shape[0]
    spare = pad - (REACH + 1) * slot_count
    all_tags = [aux_buf[place, aux_rows:].astype(jnp.float32)[0:1, :] for place in range(REACH)]
    all_tags.append(text_tags[:, :half])
    for place in range(REACH + 1):
        all_tags.append(aux_buf[place, aux_rows:].astype(jnp.float32)[8:9, :slot_count])
    if spare:
        all_tags.append(jnp.zeros((1, spare), jnp.float32))
    all_tags.append(text_tags[:, half:])
    tags = jnp.concatenate(all_tags, axis=1)
    name = lax.broadcasted_iota(jnp.int32, (DH, total), 0)
    at = lax.broadcasted_iota(jnp.int32, (DH, total), 1) - (slot_start + REACH * slot_count)
    differs = (name < OWN) & (name.astype(jnp.float32) + 1.0 != tags)
    own_slot = (name == OWN) & (at >= 0) & (at < slot_count)
    key_all[:, DH:] = jnp.where(differs | own_slot, FAR, 0.0).T.astype(jnp.bfloat16)
    scale = LOG2E * DH ** -0.5

    def turned(values):
        return values.astype(jnp.float32).T.astype(jnp.bfloat16)

    slot_end = slot_start + pad
    wide = jnp.concatenate([diagonal[...]] * together, axis=1)
    first_span = (0, slot_end, REACH * text, slot_start, wide)
    second_span = (half, total, slot_end, total, wide)

    def text_tile(group, heads, part, span):
        mine = slice(part * half, (part + 1) * half)

        def queries():
            rows_of = [text_ref[group, mine, k * DH:(k + 1) * DH] for k in heads]
            return jnp.concatenate([turned(jnp.concatenate(rows_of, axis=0)), text_mask[part]], axis=0)

        def store(result):
            result = result.astype(jnp.bfloat16)
            for number, k in enumerate(heads):
                out_ref[group, mine, k * DH:(k + 1) * DH] = result[number * half:(number + 1) * half]

        return queries, span, store

    def slot_tile(group, heads):
        extra = slot_order_ref[:, heads[0] * slot_count:(heads[-1] + 1) * slot_count]

        def queries():
            mine = pl.ds(pl.multiple_of(group * slot_count, slot_count), slot_count)
            rows_of = [slots[mine, k * DH:(k + 1) * DH] for k in heads]
            return jnp.concatenate([turned(jnp.concatenate(rows_of, axis=0)), slot_mask[...]], axis=0)

        def store(result):
            for number, k in enumerate(heads):
                kept = jnp.where(live_col[...] > 0, result[number * slot_count:(number + 1) * slot_count], 0.0)
                out_ref[group, text:, k * DH:(k + 1) * DH] = kept.astype(jnp.bfloat16)

        return queries, (text, total, slot_start, slot_end, extra), store

    vis_wait(query_parts)
    slots[...] = jnp.dot(
        placed[...], query_listed[...].reshape(n_source * vis_block, query_width), preferred_element_type=jnp.float32
    )
    score_slots, weight_slots = (score_even, score_odd), (weight_even, weight_odd)

    def one_group(group, carry):
        arrive(group, 1)
        arrive(group, 3)
        for place in range(REACH):
            key_all[place * text:(place + 1) * text, :DH] = kv_buf[group, place, :, :DH]
            val_all[:DH, place * text:(place + 1) * text] = turned(kv_buf[group, place, :, DH:])
        own = text_ref[group, :, query_width:]
        key_all[REACH * text:slot_start, :DH] = own[:half, :DH]
        val_all[:DH, REACH * text:slot_start] = turned(own[:half, DH:])
        key_all[slot_end:, :DH] = own[half:, :DH]
        val_all[:DH, slot_end:] = turned(own[half:, DH:])
        mine = pl.ds(pl.multiple_of(group * slot_count, slot_count), slot_count)
        slot_rows = [aux_buf[place, mine] for place in range(REACH + 1)]
        if spare:
            slot_rows.append(jnp.zeros((spare, 2 * DH), jnp.bfloat16))
        slot_rows = jnp.concatenate(slot_rows, axis=0)
        key_all[slot_start:slot_end, :DH] = slot_rows[:, :DH]
        val_all[:DH, slot_start:slot_end] = turned(slot_rows[:, DH:])

        tiles = []
        for head in range(0, GQ, slot_heads):
            tiles.append(slot_tile(group, range(head, head + slot_heads)))
        for head in range(0, GQ, together):
            heads = range(head, head + together)
            tiles.append(text_tile(group, heads, 0, first_span))
            tiles.append(text_tile(group, heads, 1, second_span))

        def score_steps(number):
            queries, (low, high, extra_low, extra_high, extra), _ = tiles[number]
            held = score_slots[number % 2]
            state = {"queries": queries(), "largest": None}

            def one(start_at, end_at):
                result = jnp.dot(key_all[start_at:end_at], state["queries"], preferred_element_type=jnp.float32)
                lanes = result.shape[1]
                for at in range(start_at, end_at, 128):
                    piece = result[at - start_at:at - start_at + 128]
                    if extra_low <= at < extra_high:
                        piece = piece + extra[at - extra_low:at - extra_low + 128]
                    held[at - low:at - low + 128, :lanes] = piece
                    part = jnp.max(piece.reshape(16, 8, lanes), axis=0)
                    state["largest"] = part if state["largest"] is None else jnp.maximum(state["largest"], part)

            middle = low + (high - low) // 256 * 128
            return [functools.partial(one, low, middle), functools.partial(one, middle, high)], state

        def weight_steps(number, state):
            low, high = tiles[number][1][:2]
            held, made = score_slots[number % 2], weight_slots[number % 2]
            lanes = state["largest"].shape[1]
            largest = jnp.max(state["largest"], axis=0, keepdims=True)

            def one(at, end):
                made[at:end, :lanes] = jnp.exp2((held[at:end, :lanes] - largest) * scale).astype(jnp.bfloat16)

            count = high - low
            return [functools.partial(one, at, min(at + 64, count)) for at in range(0, count, 64)], lanes

        def finish_tile(number, lanes):
            _, (low, high, *_), store = tiles[number]
            summed = jnp.dot(
                val_all[:, low:high], weight_slots[number % 2][:high - low, :lanes],
                preferred_element_type=jnp.float32,
            )
            store((summed[:DH] * (1.0 / summed[DH:DH + 1])).T)

        work, state = score_steps(0)
        for step in work:
            step()
        before = None
        for number in range(len(tiles)):
            if number == len(tiles) // 2:
                @pl.when(group + 1 < groups)
                def _():
                    relay_near(group + 1)

                @pl.when(group + 2 < groups)
                def _():
                    relay_far(group + 2)
            if before is not None:
                finish_tile(number - 1, before)
            weigh, lanes = weight_steps(number, state)
            score = []
            if number + 1 < len(tiles):
                score, state = score_steps(number + 1)
            done = 0
            for position, step in enumerate(score):
                step()
                until = (position + 1) * len(weigh) // len(score)
                for part in weigh[done:until]:
                    part()
                done = until
            for part in weigh[done:]:
                part()
            before = lanes
        finish_tile(len(tiles) - 1, before)
        return carry

    lax.fori_loop(0, groups, one_group, 0)

    for item in range(groups + 1):
        finish(item, own_copies + far_copies + near_copies)

    vis_finish(key_parts)
    vis_finish(query_parts)


def shards(mesh_shape, text_rows, vis_rows, vis_dest, segments):
    n_group, n_seq, n_shard = (mesh_shape[axis] for axis in ("group", "seq", "shard"))
    text, groups, width = text_rows.shape
    rows = segments.shape[0]
    slot_count = n_seq * CAP
    vis_count = vis_rows.shape[0]
    vis_block = up(vis_count * groups, 16)
    text_t = text_rows.transpose(1, 0, 2)
    index = np.arange(n_shard * vis_block)
    within = index % vis_block
    valid = within < vis_count * groups
    head = within % groups
    same = (head[:, None] == head[None, :]) & (index[:, None] < index[None, :]) & valid[:, None] & valid[None, :]
    place = np.arange(groups * slot_count)
    pick = (place[:, None] // slot_count == head[None, :]) & valid[None, :]
    slot = np.broadcast_to((place % slot_count)[:, None], pick.shape)

    pad = up((REACH + 1) * slot_count, 128)
    own = np.arange(pad) - REACH * slot_count
    behind = (own[:, None] > np.arange(GQ * slot_count)[None, :] % slot_count) & (own < slot_count)[:, None]
    keys = (REACH + 1) * text + pad
    aux_rows = groups * slot_count + 16
    n_source = n_seq * n_shard
    lanes = TOGETHER * (text // 2)
    vmem = pl.BlockSpec(memory_space=pltpu.VMEM)
    result = pl.pallas_call(
        functools.partial(kernel, n_group, n_seq, n_shard),
        out_shape=jax.ShapeDtypeStruct((groups, rows, GQ * DH), jnp.bfloat16),
        in_specs=[vmem] * 8,
        out_specs=vmem,
        scratch_shapes=[
            pltpu.VMEM((groups, REACH, text, 2 * DH), jnp.bfloat16),
            pltpu.VMEM((REACH + 1, aux_rows, 2 * DH), jnp.bfloat16),
            pltpu.VMEM((n_shard, vis_block, 3 * DH), jnp.bfloat16),
            pltpu.VMEM((n_source, vis_block, 3 * DH), jnp.bfloat16),
            pltpu.VMEM((n_shard, vis_block, GQ * DH), jnp.bfloat16),
            pltpu.VMEM((n_source, vis_block, GQ * DH), jnp.bfloat16),
            pltpu.VMEM((groups * slot_count, n_source * vis_block), jnp.bfloat16),
            pltpu.VMEM((keys, 2 * DH), jnp.bfloat16),
            pltpu.VMEM((DH + 16, keys), jnp.bfloat16),
            pltpu.VMEM((2, DH, lanes), jnp.bfloat16),
            pltpu.VMEM((DH, min(GQ * slot_count, lanes)), jnp.bfloat16),
            pltpu.VMEM((text // 2, text // 2), jnp.float32),
            pltpu.VMEM((groups * slot_count, GQ * DH), jnp.float32),
            pltpu.VMEM((slot_count, DH), jnp.float32),
            pltpu.VMEM((keys - text // 2, lanes), jnp.float32),
            pltpu.VMEM((keys - text // 2, lanes), jnp.float32),
            pltpu.VMEM((keys - text // 2, lanes), jnp.bfloat16),
            pltpu.VMEM((keys - text // 2, lanes), jnp.bfloat16),
            pltpu.SemaphoreType.DMA((groups + 1, 6)),
            pltpu.SemaphoreType.DMA((groups + 1, REACH)),
            pltpu.SemaphoreType.DMA((n_source,)),
            pltpu.SemaphoreType.DMA((n_source,)),
            pltpu.SemaphoreType.DMA((n_source,)),
            pltpu.SemaphoreType.DMA((n_source,)),
        ],
        compiler_params=pltpu.CompilerParams(
            collective_id=0, has_side_effects=True, vmem_limit_bytes=36 * 1024 * 1024
        ),
    )(
        text_t,
        vis_rows,
        vis_dest.reshape(vis_count),
        segments,
        jnp.asarray(same, jnp.float32),
        jnp.asarray(pick, jnp.float32),
        jnp.asarray(slot, jnp.float32),
        jnp.asarray(np.where(behind, FAR, 0.0), jnp.float32),
    )
    return result.transpose(1, 0, 2)


def solution(mesh):
    placed = (
        P(("group", "seq"), "shard", None),
        P(("group", "seq", "shard"), None, None),
        P(("group", "seq", "shard"), None),
        P(("group", "seq")),
    )
    return jax.shard_map(
        functools.partial(shards, dict(mesh.shape)),
        mesh=mesh,
        in_specs=placed,
        out_specs=P(("group", "seq"), "shard", None),
        check_vma=False,
    )
```
